512 devices in a mesh: loop: 64 (over z, x_lo, core), group: 8 (over y, x_hi).
Axes of the slice: x: 4 (x_hi: 2, x_lo: 2; x = x_hi * 2 + x_lo), y: 4, z: 16, core: 2. Of those that a mesh axis runs over, the one named last changes fastest.
Arguments:
- images: bfloat16 [65536, 1152], P(('loop', 'group')), may hold values from -0.1796875 to 0.1796875
- texts: bfloat16 [65536, 1152], P(('loop', 'group')), may hold values from -0.1796875 to 0.1796875
- image_ids: int32 [65536], P(('loop', 'group')), may hold values from 0 to 511
- text_ids: int32 [65536], P(('loop', 'group')), may hold values from 0 to 511
- logit_scale: float32 [1], replicated, may hold values from 2 to 10
- logit_bias: float32 [1], replicated, may hold values from -4 to -1
Outputs:
- image_grad: float32 [65536, 1152], P(('loop', 'group'))
- text_grad: float32 [65536, 1152], P(('loop', 'group'))
The draws below stay inside these ranges and needn't reach their ends.
All inputs are finite; a program needn't handle non-finite values.
Results may differ from the reference program's by a relative error of at most 0.0042.
Values may be sent and summed in bfloat16 or wider, within the bound.
A program may use at most 64 MiB of HBM per device.

```python
import math
import jax
import jax.numpy as jnp
from jax import lax

D = 1152
ROWS = 128
STEPS = 2
NIDS = 512
TOKENS = 65536
N_LOOP = 64
N_GROUP = 8


def with_ends(array, own_key, least, high):
    shape = array.shape
    index_at = [jax.random.randint(jax.random.fold_in(own_key, axis), (), 0, shape[axis]) for axis in range(len(shape))]
    array = array.at[tuple(index_at)].set(least)
    longest = shape.index(max(shape))
    index_at[longest] = (index_at[longest] + 1) % shape[longest]
    return array.at[tuple(index_at)].set(high)


def block_levels(own_key, dims, shards, least, largest):
    factor_of, own = 1.0, jax.random.fold_in(own_key, 6)
    for position, blocks in shards:
        steps = jnp.exp(jax.random.uniform(jax.random.fold_in(own, position), (blocks,), jnp.float32, least / len(shards), largest / len(shards)))
        factor_of = factor_of * jnp.repeat(steps, dims[position] // blocks).reshape([-1 if axis == position else 1 for axis in range(len(dims))])
    return factor_of


def noise(key, shape, deviation, bound, split=(), dtype=jnp.bfloat16):
    factor_of = block_levels(key, shape, split, -0.22, 0.18) if split else 1.0
    entries = jax.random.normal(key, shape, jnp.float32) * deviation * factor_of
    return jnp.minimum(jnp.maximum(entries, -bound), bound).astype(dtype)


def setup_inputs(seed: int = 0) -> dict:
    arg_keys = jax.random.split(jax.random.key(seed), 7)
    images = noise(arg_keys[0], (TOKENS, D), 0.03, 0.1796875, ((0, 512),))
    texts = noise(arg_keys[1], (TOKENS, D), 0.03, 0.1796875, ((0, 512),))
    image_ids = with_ends(jax.random.randint(arg_keys[2], (TOKENS,), 0, NIDS), jax.random.fold_in(arg_keys[2], 1), 0, NIDS - 1).astype(jnp.int32)
    text_ids = with_ends(jax.random.randint(arg_keys[3], (TOKENS,), 0, NIDS), jax.random.fold_in(arg_keys[3], 1), 0, NIDS - 1).astype(jnp.int32)
    logit_scale = jnp.clip(jnp.exp(jax.random.uniform(arg_keys[4], (1,), jnp.float32, math.log(2.0), math.log(10.0))), 2.0, 10.0)
    logit_bias = jnp.clip(jax.random.uniform(arg_keys[5], (1,), jnp.float32, -4.0, -1.0), -4.0, -1.0)
    return {"images": images, "texts": texts, "image_ids": image_ids, "text_ids": text_ids, "logit_scale": logit_scale, "logit_bias": logit_bias}


epsilon = 1e-06

def unit_rows(rows):
    values = rows.astype(jnp.float32)
    factor = 1.0 / jnp.sqrt(lax.optimization_barrier(jnp.sum(values * values, axis=-1, keepdims=True)) + epsilon)
    return (values * factor, factor)

def pair_terms(image_block, image_keys, text_block, text_keys, scale_value, bias_value):
    image_f = image_block.astype(jnp.float32)
    text_f = text_block.astype(jnp.float32)
    logits = scale_value * jnp.dot(image_f, text_f.T, precision=lax.Precision.HIGHEST) + bias_value
    labels = jnp.where(image_keys[:, None] == text_keys[None, :], 1.0, -1.0).astype(jnp.float32)
    weights = (-labels * jax.nn.sigmoid(-labels * logits)).astype(jnp.bfloat16).astype(jnp.float32)
    image_part = scale_value * jnp.dot(weights, text_f, precision=lax.Precision.HIGHEST)
    text_part = scale_value * jnp.dot(weights.T, image_f, precision=lax.Precision.HIGHEST)
    return (image_part, text_part)

def unit_backward(grad_unit, direction, factor):
    along = lax.optimization_barrier(jnp.sum(direction * grad_unit, axis=-1, keepdims=True))
    return factor * (grad_unit - direction * along)

def reference(images, texts, image_ids, text_ids, logit_scale, logit_bias):
    width = N_GROUP * ROWS
    image_dir, image_factor = unit_rows(images)
    text_dir, text_factor = unit_rows(texts)
    image_unit = image_dir.astype(jnp.bfloat16).reshape(N_LOOP, width, D)
    text_unit = text_dir.astype(jnp.bfloat16).reshape(N_LOOP, width, D)
    image_keys = image_ids.reshape(N_LOOP, width)
    text_keys = text_ids.reshape(N_LOOP, width)
    scale_value = logit_scale[0]
    bias_value = logit_bias[0]
    image_total = jnp.zeros((N_LOOP, width, D), jnp.float32)
    text_total = jnp.zeros((N_LOOP, width, D), jnp.float32)
    for offset in range(STEPS + 1):
        moved_images = jnp.roll(image_unit, -offset, axis=0)
        moved_keys = jnp.roll(image_keys, -offset, axis=0)

        def one_block(items):
            return pair_terms(items[0], items[1], items[2], items[3], scale_value, bias_value)
        image_part, text_part = lax.map(one_block, (moved_images, moved_keys, text_unit, text_keys))
        image_total = image_total + jnp.roll(image_part, offset, axis=0)
        text_total = text_total + text_part
    image_grad = unit_backward(image_total.reshape(TOKENS, D), image_dir, image_factor)
    text_grad = unit_backward(text_total.reshape(TOKENS, D), text_dir, text_factor)
    return (image_grad, text_grad)
```

```python
import functools

import jax
import jax.numpy as jnp
from jax import lax
from jax.experimental import pallas as pl
from jax.experimental.pallas import tpu as pltpu
from jax.sharding import PartitionSpec as P

epsilon = 1e-06
CHUNKS = 3
MESH = pl.DeviceIdType.MESH
F32, BF16 = jnp.float32, jnp.bfloat16


def kernel(
    n_loop, images, texts, image_ids, text_ids, scale, bias, image_out, text_out,
    img, txt, idi, idt, w, wt, gt, gi, oc_s, oc_r, z_s, z_r, d_s, d_r, x_s, x_r, h_s, h_r, y_s, y_r,
    gx_s, gx_r, gf_s, gf_r, gz_s, gz_r, go_s, go_r, gy_s, gy_r, gh_s, gh_r, id_s, id_r,
    ro_s, ro_r, rz_s, rz_r, rd_s, rd_r, rx_s, rx_r, rh_s, rh_r, ry_s, ry_r,
):
    R = images.shape[0]
    H = R // 2
    D = images.shape[1]
    C = CHUNKS
    DC = D // C
    loop, group = lax.axis_index("loop"), lax.axis_index("group")
    core = lax.rem(loop, 2)
    x_lo = lax.rem(loop // 2, 2)
    y, x_hi = group // 2, lax.rem(group, 2)
    flip = loop + 2 - 4 * x_lo
    other = (loop + 1 - 2 * core, group)
    near_a = (flip, group)
    near_b = (flip, group + 1 - 2 * x_hi)
    y_up = (loop, lax.rem(y + 1, 4) * 2 + x_hi)
    y_down = (loop, lax.rem(y + 3, 4) * 2 + x_hi)
    z_up = (lax.rem(loop + 4, n_loop), group)
    z_down = (lax.rem(loop + n_loop - 4, n_loop), group)
    x_near = (near_a, near_b)
    y_near = (y_up, y_down)
    low = x_lo == 0
    mine = 6 - 2 * x_lo
    theirs = 4 + 2 * x_lo

    barrier = pltpu.get_barrier_semaphore()
    for device in (other, near_a, near_b, y_up, y_down):
        pl.semaphore_signal(barrier, inc=1, device_id=device, device_id_type=MESH)

    @pl.when(low)
    def _():
        for device in (z_up, z_down):
            pl.semaphore_signal(barrier, inc=1, device_id=device, device_id_type=MESH)

    def normalize(rows, block):
        values = rows[...].astype(F32)
        factor = 1.0 / jnp.sqrt(jnp.sum(values * values, axis=-1, keepdims=True) + epsilon)
        for ch in range(C):
            block[ch, 0:R, :] = (values[:, ch * DC:(ch + 1) * DC] * factor).astype(BF16)

    normalize(texts, txt)
    idt[0] = text_ids[...]
    idi[0] = image_ids[...]
    pl.semaphore_wait(barrier, 7 - 2 * x_lo)

    def rows_of(slot, count=1):
        return pl.ds(pl.multiple_of(slot * R, R), count * R)

    def send(src, dst, s, r, device):
        return pltpu.make_async_remote_copy(
            src_ref=src, dst_ref=dst, send_sem=s, recv_sem=r, device_id=device, device_id_type=MESH)

    def gx(ch, i):
        return send(txt.at[ch, 0:R], txt.at[ch, rows_of(theirs + i)], gx_s.at[i, ch], gx_r.at[i, ch], x_near[i])

    def gf(ch, i):
        return send(txt.at[ch, pl.ds(pl.multiple_of((mine + i) * R + i * H, H), H)],
                    txt.at[ch, R + i * H:R + (i + 1) * H], gf_s.at[i, ch], gf_r.at[i, ch], x_near[1 - i])

    def gz(ch, i):
        return send(txt.at[ch, (6 + i) * R:(7 + i) * R], txt.at[ch, (4 + i) * R:(5 + i) * R],
                    gz_s.at[i, ch], gz_r.at[i, ch], z_up)

    def go(ch, i):
        return send(txt.at[ch, rows_of(4 * core + i)], txt.at[ch, (2 + i) * R:(3 + i) * R],
                    go_s.at[i, ch], go_r.at[i, ch], other)

    def gy(ch, i):
        return send(img.at[ch, 0:R], img.at[ch, (1 + i) * R:(2 + i) * R], gy_s.at[i, ch], gy_r.at[i, ch], y_near[i])

    def gh(ch, i):
        return send(img.at[ch, (1 + i) * R + i * H:(1 + i) * R + (i + 1) * H],
                    img.at[ch, 3 * R + i * H:3 * R + (i + 1) * H], gh_s.at[i, ch], gh_r.at[i, ch], y_near[i])

    id_x = [send(idt.at[0], idt.at[theirs + i], id_s.at[i], id_r.at[i], x_near[i]) for i in range(2)]
    id_f = send(idt.at[mine], idt.at[1], id_s.at[2], id_r.at[2], near_b)
    id_z = send(idt.at[6:8], idt.at[4:6], id_s.at[3], id_r.at[3], z_up)
    id_o = send(idt.at[pl.ds(4 * core, 2)], idt.at[2:4], id_s.at[4], id_r.at[4], other)
    id_y = [send(idi.at[0], idi.at[1 + i], id_s.at[5 + i], id_r.at[5 + i], y_near[i]) for i in range(2)]
    id_h = send(idi.at[1], idi.at[3], id_s.at[7], id_r.at[7], y_up)

    for ch in range(C):
        for i in range(2):
            gx(ch, i).start()
    for copy in id_x:
        copy.start()
    normalize(images, img)
    for ch in range(C):
        for i in range(2):
            gy(ch, i).start()
    for copy in id_y:
        copy.start()

    @pl.when(core == 0)
    def _():
        for ch in range(C):
            go(ch, 0).start()

    for ch in range(C):
        for i in range(2):
            gx(ch, i).wait_recv()

            @pl.when(low)
            def _():
                gz(ch, i).start()

            gf(ch, i).start()

            @pl.when((x_lo == 1) & (core == 1))
            def _():
                go(ch, i).start()

        for i in range(2):
            gy(ch, i).wait_recv()
            gh(ch, i).start()
    for copy in id_x:
        copy.wait_recv()
    id_f.start()

    @pl.when(low)
    def _():
        id_z.start()

    for copy in id_y:
        copy.wait_recv()
    id_h.start()
    id_f.wait_recv()

    @pl.when(low)
    def _():
        id_z.wait_recv()

    id_o.start()

    for ch in range(C):
        for i in range(2):
            gf(ch, i).wait_recv()

        @pl.when(core == 0)
        def _():
            go(ch, 1).start()

        @pl.when(low)
        def _():
            for i in range(2):
                gz(ch, i).wait_recv()

        @pl.when(low & (core == 1))
        def _():
            for i in range(2):
                go(ch, i).start()

        for i in range(2):
            gh(ch, i).wait_recv()
    id_h.wait_recv()
    id_o.wait_recv()
    for ch in range(C):
        for i in range(2):
            go(ch, i).wait_recv()

    image_keys = jnp.concatenate(
        [jnp.transpose(jnp.broadcast_to(idi[s], (128, R)))[:, 0:1] for s in range(4)], axis=0)
    scale_value, bias_value = scale[0], bias[0]

    def weigh(j, carry):
        rows = pl.ds(pl.multiple_of(j * 2 * R, 2 * R), 2 * R)
        dots = None
        for ch in range(C):
            part = lax.dot_general(
                img[ch], txt[ch, rows, :], (((1,), (1,)), ((), ())), preferred_element_type=F32)
            dots = part if dots is None else dots + part
        logits = scale_value * dots + bias_value
        text_keys = jnp.concatenate([idt[2 * j], idt[2 * j + 1]], axis=1)
        same = image_keys == text_keys
        share = jax.nn.sigmoid(jnp.where(same, -logits, logits))
        weights = jnp.where(same, -share, share)
        w[j] = weights.astype(BF16)
        wt[j] = jnp.transpose(weights).astype(BF16)
        return carry

    lax.fori_loop(0, 3, weigh, 0)

    def ro(ch):
        return send(oc_s.at[ch], oc_r.at[ch], ro_s.at[ch], ro_r.at[ch], other)

    def rz(ch):
        return send(z_s.at[ch], z_r.at[ch], rz_s.at[ch], rz_r.at[ch], z_down)

    def rd(ch, i):
        return send(d_s.at[ch, i * H:(i + 1) * H], d_r.at[ch, i * H:(i + 1) * H],
                    rd_s.at[i, ch], rd_r.at[i, ch], x_near[i])

    def rx(ch, i):
        return send(x_s.at[ch, i], x_r.at[ch, i], rx_s.at[i, ch], rx_r.at[i, ch], x_near[i])

    def rh(ch, i):
        return send(h_s.at[ch, i * H:(i + 1) * H], h_r.at[ch, i * H:(i + 1) * H],
                    rh_s.at[i, ch], rh_r.at[i, ch], y_near[i])

    def ry(ch, i):
        return send(y_s.at[ch, i], y_r.at[ch, i], ry_s.at[i, ch], ry_r.at[i, ch], y_near[i])

    for ch in range(C):
        def text_part(j, carry, ch=ch):
            rows = pl.ds(pl.multiple_of(j * 2 * R, 2 * R), 2 * R)
            gt[ch, rows, :] = jnp.dot(wt[j], img[ch], preferred_element_type=F32)
            return carry

        lax.fori_loop(0, 3, text_part, 0)
        oc_s[ch] = gt[ch, 2 * R:4 * R, :].astype(BF16)
        ro(ch).start()

        def image_part(i, carry, ch=ch):
            rows = pl.ds(pl.multiple_of(i * 2 * R, 2 * R), 2 * R)
            total = None
            for j in range(3):
                part = jnp.dot(w[j, rows, :], txt[ch, 2 * j * R:2 * (j + 1) * R, :], preferred_element_type=F32)
                total = part if total is None else total + part
            gi[ch, rows, :] = total
            return carry

        lax.fori_loop(0, 2, image_part, 0)
        h_s[ch] = gi[ch, 3 * R:4 * R, :].astype(BF16)
        for i in range(2):
            rh(ch, i).start()

    for ch in range(C):
        ro(ch).wait_recv()
        at = pl.ds(pl.multiple_of(4 * core * R, 2 * R), 2 * R)
        gt[ch, at, :] = gt[ch, at, :] + oc_r[ch].astype(F32)

        @pl.when(low)
        def _():
            z_s[ch] = gt[ch, 4 * R:6 * R, :].astype(BF16)
            rz(ch).start()

        d_s[ch] = gt[ch, R:2 * R, :].astype(BF16)
        for i in range(2):
            rd(ch, i).start()
        for i in range(2):
            rh(ch, i).wait_recv()
        y_s[ch, 0, 0:H] = (gi[ch, 2 * R:2 * R + H, :] + h_r[ch, 0:H].astype(F32)).astype(BF16)
        y_s[ch, 0, H:R] = gi[ch, 2 * R + H:3 * R, :].astype(BF16)
        y_s[ch, 1, 0:H] = gi[ch, R:R + H, :].astype(BF16)
        y_s[ch, 1, H:R] = (gi[ch, R + H:2 * R, :] + h_r[ch, H:R].astype(F32)).astype(BF16)
        for i in range(2):
            ry(ch, i).start()

    for ch in range(C):
        @pl.when(low)
        def _():
            rz(ch).wait_recv()
            gt[ch, 4 * R:6 * R, :] = z_r[ch].astype(F32)

        for i in range(2):
            rd(ch, i).wait_recv()
        x_s[ch, 0, 0:H] = gt[ch, 4 * R:4 * R + H, :].astype(BF16)
        x_s[ch, 0, H:R] = (gt[ch, 4 * R + H:5 * R, :] + d_r[ch, H:R].astype(F32)).astype(BF16)
        x_s[ch, 1, 0:H] = (gt[ch, 5 * R:5 * R + H, :] + d_r[ch, 0:H].astype(F32)).astype(BF16)
        x_s[ch, 1, H:R] = gt[ch, 5 * R + H:6 * R, :].astype(BF16)
        for i in range(2):
            rx(ch, i).start()

    def backward(rows, parts, out):
        values = rows[...].astype(F32)
        factor = 1.0 / jnp.sqrt(jnp.sum(values * values, axis=-1, keepdims=True) + epsilon)
        unit = values * factor
        grad = scale_value * jnp.concatenate(parts, axis=-1)
        along = jnp.sum(unit * grad, axis=-1, keepdims=True)
        out[...] = factor * (grad - unit * along)

    for ch in range(C):
        for i in range(2):
            ry(ch, i).wait_recv()
    backward(images, [gi[ch, 0:R, :] + (y_r[ch, 0].astype(F32) + y_r[ch, 1].astype(F32)) for ch in range(C)],
             image_out)
    for ch in range(C):
        for i in range(2):
            rx(ch, i).wait_recv()
    backward(texts, [gt[ch, 0:R, :] + (x_r[ch, 0].astype(F32) + x_r[ch, 1].astype(F32)) for ch in range(C)],
             text_out)

    for ch in range(C):
        for i in range(2):
            for copy in (gx, gf, go, gy, gh, rd, rx, rh, ry):
                copy(ch, i).wait_send()
        ro(ch).wait_send()
    for copy in id_x + id_y + [id_f, id_o, id_h]:
        copy.wait_send()

    @pl.when(low)
    def _():
        id_z.wait_send()
        for ch in range(C):
            rz(ch).wait_send()
            for i in range(2):
                gz(ch, i).wait_send()


def shards(n_loop, images, texts, image_ids, text_ids, logit_scale, logit_bias):
    R, D = images.shape
    C = CHUNKS
    DC = D // C
    dma = pltpu.SemaphoreType.DMA
    vmem = pl.BlockSpec(memory_space=pltpu.VMEM)
    smem = pl.BlockSpec(memory_space=pltpu.SMEM)
    pair = lambda: [dma((2, C)), dma((2, C))]
    single = lambda: [dma((C,)), dma((C,))]
    return pl.pallas_call(
        functools.partial(kernel, n_loop),
        out_shape=(jax.ShapeDtypeStruct((R, D), F32), jax.ShapeDtypeStruct((R, D), F32)),
        in_specs=[vmem, vmem, vmem, vmem, smem, smem],
        out_specs=(vmem, vmem),
        scratch_shapes=[
            pltpu.VMEM((C, 4 * R, DC), BF16),
            pltpu.VMEM((C, 8 * R, DC), BF16),
            pltpu.VMEM((4, 1, R), jnp.int32),
            pltpu.VMEM((8, 1, R), jnp.int32),
            pltpu.VMEM((3, 4 * R, 2 * R), BF16),
            pltpu.VMEM((3, 2 * R, 4 * R), BF16),
            pltpu.VMEM((C, 6 * R, DC), F32),
            pltpu.VMEM((C, 4 * R, DC), F32),
            pltpu.VMEM((C, 2 * R, DC), BF16),
            pltpu.VMEM((C, 2 * R, DC), BF16),
            pltpu.VMEM((C, 2 * R, DC), BF16),
            pltpu.VMEM((C, 2 * R, DC), BF16),
            pltpu.VMEM((C, R, DC), BF16),
            pltpu.VMEM((C, R, DC), BF16),
            pltpu.VMEM((C, 2, R, DC), BF16),
            pltpu.VMEM((C, 2, R, DC), BF16),
            pltpu.VMEM((C, R, DC), BF16),
            pltpu.VMEM((C, R, DC), BF16),
            pltpu.VMEM((C, 2, R, DC), BF16),
            pltpu.VMEM((C, 2, R, DC), BF16),
        ] + pair() + pair() + pair() + pair() + pair() + pair() + [dma((8,)), dma((8,))]
        + single() + single() + pair() + pair() + pair() + pair(),
        compiler_params=pltpu.CompilerParams(
            collective_id=0, has_side_effects=True, vmem_limit_bytes=48 * 1024 * 1024),
        cost_estimate=pl.CostEstimate(
            flops=6 * 4 * R * 6 * R * D, bytes_accessed=12 * R * D, transcendentals=24 * R * R),
    )(images, texts, image_ids.reshape(1, R), text_ids.reshape(1, R), logit_scale, logit_bias)


def solution(mesh):
    rows = P(("loop", "group"), None)
    ids = P(("loop", "group"))
    return jax.shard_map(
        functools.partial(shards, mesh.shape["loop"]), mesh=mesh,
        in_specs=(rows, rows, ids, ids, P(), P()), out_specs=(rows, rows), check_vma=False)
```

```python
import functools

import jax
import jax.numpy as jnp
from jax import lax
from jax.experimental import pallas as pl
from jax.experimental.pallas import tpu as pltpu
from jax.sharding import PartitionSpec as P

epsilon = 1e-06
MESH = pl.DeviceIdType.MESH
F32, BF16 = jnp.float32, jnp.bfloat16
TILE = 384


def kernel(
    n_loop, images, texts, image_ids, text_ids, scale, bias, image_out, text_out,
    raw_i, raw_t, img, txt, idi, idt, keys, w, wt, gt, gi,
    oc_s, oc_r, d_s, d_r, c_s, c_r, z_r, x_s, x_r, h_s, h_r, y_s, y_r,
    load, gx_s, gx_r, g2_s, g2_r, gf_s, gf_r, gz_s, gz_r, go_s, go_r, gy_s, gy_r, gw_s, gw_r, gh_s, gh_r, id_s, id_r,
    ro_s, ro_r, rd_s, rd_r, rc_s, rc_r, rz_s, rz_r, rx_s, rx_r, rh_s, rh_r, rn_s, rn_r, ra_s, ra_r,
):
    R, D = raw_i.shape
    H = R // 2
    loop, group = lax.axis_index("loop"), lax.axis_index("group")
    core = lax.rem(loop, 2)
    x_lo = lax.rem(loop // 2, 2)
    y, x_hi = group // 2, lax.rem(group, 2)
    flip = loop + 2 - 4 * x_lo
    other = (loop + 1 - 2 * core, group)
    x_near = ((flip, group), (flip, group + 1 - 2 * x_hi))
    y_near = ((loop, lax.rem(y + 1, 4) * 2 + x_hi), (loop, lax.rem(y + 3, 4) * 2 + x_hi))
    z_up = (lax.rem(loop + 4, n_loop), group)
    z_down = (lax.rem(loop + n_loop - 4, n_loop), group)
    low, high = x_lo == 0, x_lo == 1

    loads = [
        pltpu.make_async_copy(src, dst, load.at[i])
        for i, (src, dst) in enumerate(
            [(texts, raw_t), (images, raw_i), (text_ids, idt.at[0]), (image_ids, idi.at[0])])
    ]
    for copy in loads:
        copy.start()
    barrier = pltpu.get_barrier_semaphore()
    for device in (*x_near, *y_near, z_down, other):
        pl.semaphore_signal(barrier, inc=1, device_id=device, device_id_type=MESH)

    def normalize(rows, block):
        values = rows[...].astype(F32)
        factor = 1.0 / jnp.sqrt(jnp.sum(values * values, axis=-1, keepdims=True) + epsilon)
        block[0:R, :] = (values * factor).astype(BF16)

    def send(src, dst, s, r, device):
        return pltpu.make_async_remote_copy(
            src_ref=src, dst_ref=dst, send_sem=s, recv_sem=r, device_id=device, device_id_type=MESH)

    def half(ref, slot, h):
        at = slot * R + h * H
        return ref.at[pl.ds(at if isinstance(at, int) else pl.multiple_of(at, H), H)]

    def block(ref, slot):
        at = slot * R
        return ref.at[pl.ds(at if isinstance(at, int) else pl.multiple_of(at, R), R)]

    def gx(i):
        return send(half(txt, 0, i), half(txt, 4 + 2 * x_lo + i, i), gx_s.at[i], gx_r.at[i], x_near[i])

    def g2(i):
        return send(half(txt, 6 * x_lo, 1 - i), half(txt, 4 + i, 1 - i), g2_s.at[i], g2_r.at[i], x_near[i])

    def gf(i):
        return send(half(txt, 6 - 2 * x_lo + i, i), half(txt, 1, i), gf_s.at[i], gf_r.at[i], x_near[1 - i])

    def gz(i):
        return send(half(txt, (6 + i) * (1 - x_lo), i), half(txt, 4 + i + x_lo * (2 - i), i),
                    gz_s.at[i], gz_r.at[i], z_up)

    def go(i):
        return send(block(txt, 4 * core + i), block(txt, 2 + i), go_s.at[i], go_r.at[i], other)

    def gy(i):
        return send(half(img, 0, i), half(img, 1 + i, i), gy_s.at[i], gy_r.at[i], y_near[i])

    def gw(i):
        return send(half(img, 0, 1 - i), half(img, 1 + i, 1 - i), gw_s.at[i], gw_r.at[i], y_near[i])

    def gh(i):
        return send(half(img, 1 + i, i), half(img, 3, i), gh_s.at[i], gh_r.at[i], y_near[i])

    def ids(k, src, dst, device):
        return send(src, dst, id_s.at[k], id_r.at[k], device)

    id_x = [ids(i, idt.at[0], idt.at[4 + 2 * x_lo + i], x_near[i]) for i in range(2)]
    id_f = ids(2, idt.at[6 - 2 * x_lo], idt.at[1], x_near[1])
    id_z = ids(3, idt.at[6:8], idt.at[4:6], z_up)
    id_o = ids(4, idt.at[pl.ds(4 * core, 2)], idt.at[2:4], other)
    id_y = [ids(5 + i, idi.at[0], idi.at[1 + i], y_near[i]) for i in range(2)]
    id_h = ids(7, idi.at[1], idi.at[3], y_near[0])

    loads[0].wait()
    normalize(raw_t, txt)
    loads[2].wait()
    loads[3].wait()
    pl.semaphore_wait(barrier, 6)
    for i in range(2):
        gx(i).start()

    @pl.when(low)
    def _():
        for i in range(2):
            g2(i).start()

    @pl.when(high)
    def _():
        for i in range(2):
            gz(i).start()

    loads[1].wait()
    normalize(raw_i, img)
    for i in range(2):
        gy(i).start()
    for i in range(2):
        gw(i).start()
    for copy in id_x + id_y:
        copy.start()

    @pl.when(core == 0)
    def _():
        go(0).start()

    for i in range(2):
        gx(i).wait_recv()
        gf(i).start()

        @pl.when(low)
        def _():
            gz(i).start()

    for i in range(2):
        gy(i).wait_recv()
        gh(i).start()

    @pl.when(high)
    def _():
        for i in range(2):
            gz(i).wait_recv()
            g2(1 - i).start()

    for copy in id_x + id_y:
        copy.wait_recv()
    id_f.start()
    id_h.start()

    @pl.when(low)
    def _():
        id_z.start()
        id_z.wait_recv()

    id_f.wait_recv()
    id_o.start()

    for i in range(2):
        gw(i).wait_recv()
    for i in range(2):
        g2(i).wait_recv()

        @pl.when(low)
        def _():
            gz(i).wait_recv()

        @pl.when(core == 1)
        def _():
            go(i).start()

    for i in range(2):
        gf(i).wait_recv()

    @pl.when(core == 0)
    def _():
        go(1).start()

    id_h.wait_recv()
    for s in range(4):
        keys[s * R:(s + 1) * R, :] = jnp.transpose(jnp.broadcast_to(idi[s], (128, R)))
    id_o.wait_recv()
    for i in range(2):
        gh(i).wait_recv()

    scale_value, bias_value = scale[0], bias[0]

    def weigh(b):
        def body(a, carry):
            rows = pl.ds(pl.multiple_of(a * 2 * R, 2 * R), 2 * R)
            dots = lax.dot_general(
                img[rows, :], txt[b * 2 * R:(b + 1) * 2 * R, :], (((1,), (1,)), ((), ())), preferred_element_type=F32)
            logits = scale_value * dots + bias_value
            mine = keys[rows, :]
            same = jnp.concatenate([mine == idt[2 * b], mine == idt[2 * b + 1]], axis=1)
            share = jax.nn.sigmoid(jnp.where(same, -logits, logits))
            weights = jnp.where(same, -share, share)
            w[rows, b * 2 * R:(b + 1) * 2 * R] = weights.astype(BF16)
            wt[b * 2 * R:(b + 1) * 2 * R, rows] = jnp.transpose(weights).astype(BF16)
            return carry

        lax.fori_loop(0, 2, body, 0)

    weigh(0)
    weigh(2)
    for i in range(2):
        go(i).wait_recv()
    weigh(1)

    def ro(i):
        return send(block(oc_s, i), block(oc_r, i), ro_s.at[i], ro_r.at[i], other)

    def rd(i):
        return send(half(d_s, 0, i), half(d_r, 0, i), rd_s.at[i], rd_r.at[i], x_near[1 - i])

    def rc(i):
        return send(half(c_s, i, 1 - i), half(c_r, 0, 1 - i), rc_s.at[i], rc_r.at[i], x_near[i])

    def rz(i):
        return send(half(c_s, i, i), half(z_r, 0, i), rz_s.at[i], rz_r.at[i], z_down)

    def rz_on(i):
        return send(half(c_r, 0, i), half(z_r, 0, i), rz_s.at[i], rz_r.at[i], z_down)

    def rx(i):
        return send(half(x_s, 0, i), half(x_r, 0, i), rx_s.at[i], rx_r.at[i], x_near[i])

    def rh(i):
        return send(half(h_s, 0, i), half(h_r, 0, i), rh_s.at[i], rh_r.at[i], y_near[i])

    def rn(i):
        return send(half(y_s, i, 1 - i), half(y_r, i, 1 - i), rn_s.at[i], rn_r.at[i], y_near[i])

    def ra(i):
        return send(half(y_s, i, i), half(y_r, i, i), ra_s.at[i], ra_r.at[i], y_near[i])

    def text_part(b, store):
        def body(n, carry):
            cols = pl.ds(pl.multiple_of(n * TILE, TILE), TILE)
            rows = pl.ds(b * 2 * R if isinstance(b, int) else pl.multiple_of(b * 2 * R, 2 * R), 2 * R)
            store(cols, jnp.dot(wt[rows, :], img[:, cols], preferred_element_type=F32))
            return carry

        lax.fori_loop(0, D // TILE, body, 0)

    def image_part(a, store):
        def body(n, carry):
            cols = pl.ds(pl.multiple_of(n * TILE, TILE), TILE)
            store(cols, jnp.dot(w[a * 2 * R:(a + 1) * 2 * R, :], txt[0:6 * R, cols], preferred_element_type=F32))
            return carry

        lax.fori_loop(0, D // TILE, body, 0)

    def keep_other(cols, part):
        oc_s[:, cols] = part.astype(BF16)

    text_part(1, keep_other)
    for i in range(2):
        ro(i).start()

    def keep_far(cols, part):
        h_s[:, cols] = part[R:2 * R].astype(BF16)
        gi[2 * R:3 * R, cols] = part[0:R]
        y_s[H:R, cols] = part[H:R].astype(BF16)

    image_part(1, keep_far)
    for i in range(2):
        rh(i).start()
    rn(0).start()

    def keep_near(cols, part):
        gi[0:2 * R, cols] = part
        y_s[R:R + H, cols] = part[R:R + H].astype(BF16)

    image_part(0, keep_near)
    rn(1).start()

    def keep_text(b):
        def store(cols, part):
            gt[pl.ds(pl.multiple_of(b * 2 * R, 2 * R), 2 * R), cols] = part

        return store

    text_part(2 * (1 - core), keep_text(1 - core))
    text_part(2 * core, keep_text(core))
    for i in range(2):
        ro(i).wait_recv()
    at = pl.ds(pl.multiple_of(core * 2 * R, 2 * R), 2 * R)
    gt[at, :] = gt[at, :] + oc_r[...].astype(F32)
    c_s[...] = gt[2 * R:4 * R, :].astype(BF16)
    for i in range(2):
        rc(i).start()

    @pl.when(low)
    def _():
        for i in range(2):
            rz(i).start()

    d_s[...] = gt[R:2 * R, :].astype(BF16)
    for i in range(2):
        rd(i).start()

    for i in range(2):
        rh(i).wait_recv()
        y_s[i * R + i * H:i * R + (i + 1) * H, :] = (
            gi[(2 - i) * R + i * H:(2 - i) * R + (i + 1) * H, :] + h_r[i * H:(i + 1) * H, :].astype(F32)).astype(BF16)
        ra(i).start()

    for i in range(2):
        rc(i).wait_recv()

    @pl.when(high)
    def _():
        for i in range(2):
            rz_on(i).start()

    @pl.when(low)
    def _():
        for i in range(2):
            rz(i).wait_recv()
            gt[(2 + i) * R + i * H:(2 + i) * R + (i + 1) * H, :] = z_r[i * H:(i + 1) * H, :].astype(F32)

    for i in range(2):
        rd(i).wait_recv()
        x_s[i * H:(i + 1) * H, :] = (
            gt[(2 + i) * R + i * H:(2 + i) * R + (i + 1) * H, :] + d_r[i * H:(i + 1) * H, :].astype(F32)).astype(BF16)
        rx(i).start()

    def backward(rows, total, out):
        values = rows[...].astype(F32)
        factor = 1.0 / jnp.sqrt(jnp.sum(values * values, axis=-1, keepdims=True) + epsilon)
        unit = values * factor
        grad = scale_value * total
        along = jnp.sum(unit * grad, axis=-1, keepdims=True)
        out[...] = factor * (grad - unit * along)

    for i in range(2):
        rn(i).wait_recv()
        ra(i).wait_recv()
    backward(raw_i, gi[0:R, :] + (y_r[0:R, :].astype(F32) + y_r[R:2 * R, :].astype(F32)), image_out)

    @pl.when(high)
    def _():
        for i in range(2):
            rz(i).wait_recv()
        gt[R:2 * R, :] = gt[0:R, :] + z_r[...].astype(F32)

    @pl.when(low)
    def _():
        gt[R:2 * R, :] = gt[0:R, :] + c_r[...].astype(F32)

    for i in range(2):
        rx(i).wait_recv()
    backward(raw_t, gt[R:2 * R, :] + x_r[...].astype(F32), text_out)

    for i in range(2):
        for copy in (gx, g2, gf, gz, go, gy, gw, gh, ro, rd, rc, rz, rx, rh, rn, ra):
            copy(i).wait_send()
    for copy in id_x + id_y + [id_f, id_o, id_h]:
        copy.wait_send()

    @pl.when(low)
    def _():
        id_z.wait_send()


def shards(n_loop, images, texts, image_ids, text_ids, logit_scale, logit_bias):
    R, D = images.shape
    dma = pltpu.SemaphoreType.DMA
    vmem = pl.BlockSpec(memory_space=pltpu.VMEM)
    smem = pl.BlockSpec(memory_space=pltpu.SMEM)
    anywhere = pl.BlockSpec(memory_space=pl.ANY)

    def rows(count, dtype=BF16):
        return pltpu.VMEM((count * R, D), dtype)

    return pl.pallas_call(
        functools.partial(kernel, n_loop),
        out_shape=(jax.ShapeDtypeStruct((R, D), F32), jax.ShapeDtypeStruct((R, D), F32)),
        in_specs=[anywhere, anywhere, anywhere, anywhere, smem, smem],
        out_specs=(vmem, vmem),
        scratch_shapes=[
            rows(1), rows(1), rows(4), rows(8),
            pltpu.VMEM((4, 1, R), jnp.int32), pltpu.VMEM((8, 1, R), jnp.int32), pltpu.VMEM((4 * R, 128), jnp.int32),
            pltpu.VMEM((4 * R, 6 * R), BF16), pltpu.VMEM((6 * R, 4 * R), BF16), rows(4, F32), rows(3, F32),
            rows(2), rows(2), rows(1), rows(1), rows(2), rows(1), rows(1), rows(1), rows(1), rows(1), rows(1),
            rows(2), rows(2), dma((4,)),
        ] + [dma((2,))] * 16 + [dma((8,))] * 2 + [dma((2,))] * 16,
        compiler_params=pltpu.CompilerParams(
            collective_id=0, has_side_effects=True, vmem_limit_bytes=56 * 1024 * 1024),
        cost_estimate=pl.CostEstimate(
            flops=6 * 4 * R * 6 * R * D, bytes_accessed=12 * R * D, transcendentals=24 * R * R),
    )(images, texts, image_ids.reshape(1, R), text_ids.reshape(1, R), logit_scale, logit_bias)


def solution(mesh):
    rows = P(("loop", "group"), None)
    ids = P(("loop", "group"))
    return jax.shard_map(
        functools.partial(shards, mesh.shape["loop"]), mesh=mesh,
        in_specs=(rows, rows, ids, ids, P(), P()), out_specs=(rows, rows), check_vma=False)
```

```python
import functools

import jax
import jax.numpy as jnp
from jax import lax
from jax.experimental import pallas as pl
from jax.experimental.pallas import tpu as pltpu
from jax.sharding import PartitionSpec as P

epsilon = 1e-06
MESH = pl.DeviceIdType.MESH
F32, BF16 = jnp.float32, jnp.bfloat16
ROWS_AT_ONCE = 256


def kernel(
    n_loop, images, texts, image_ids, text_ids, scale, bias, image_out, text_out,
    raw_i, raw_t, img, txt, idi, idt, keys, w, wt, gt, gi,
    t_s, oc_r, d_s, d_r, c_r, z_r, x_s, x_r, h_s, h_r, y_s, y_r,
    load, gx_s, gx_r, g2_s, g2_r, gf_s, gf_r, gz_s, gz_r, go_s, go_r, gy_s, gy_r, gw_s, gw_r, gh_s, gh_r, id_s, id_r,
    ro_s, ro_r, rd_s, rd_r, rc_s, rc_r, rz_s, rz_r, rx_s, rx_r, rh_s, rh_r, rn_s, rn_r, ra_s, ra_r,
):
    R, D = raw_i.shape
    H = R // 2
    loop, group = lax.axis_index("loop"), lax.axis_index("group")
    core = lax.rem(loop, 2)
    x_lo = lax.rem(loop // 2, 2)
    y, x_hi = group // 2, lax.rem(group, 2)
    flip = loop + 2 - 4 * x_lo
    other = (loop + 1 - 2 * core, group)
    x_near = ((flip, group), (flip, group + 1 - 2 * x_hi))
    y_near = ((loop, lax.rem(y + 1, 4) * 2 + x_hi), (loop, lax.rem(y + 3, 4) * 2 + x_hi))
    z_up = (lax.rem(loop + 4, n_loop), group)
    z_down = (lax.rem(loop + n_loop - 4, n_loop), group)
    low, high = x_lo == 0, x_lo == 1

    loads = [
        pltpu.make_async_copy(src, dst, load.at[i])
        for i, (src, dst) in enumerate(
            [(texts, raw_t), (images, raw_i), (text_ids, idt.at[0]), (image_ids, idi.at[0])])
    ]
    for copy in loads:
        copy.start()
    barrier = pltpu.get_barrier_semaphore()
    for device in (*x_near, *y_near, z_down, other):
        pl.semaphore_signal(barrier, inc=1, device_id=device, device_id_type=MESH)

    def normalize(rows, block):
        values = rows[...].astype(F32)
        factor = 1.0 / jnp.sqrt(jnp.sum(values * values, axis=-1, keepdims=True) + epsilon)
        block[0:R, :] = (values * factor).astype(BF16)

    def send(src, dst, s, r, device):
        return pltpu.make_async_remote_copy(
            src_ref=src, dst_ref=dst, send_sem=s, recv_sem=r, device_id=device, device_id_type=MESH)

    def half(ref, slot, h):
        at = slot * R + h * H
        return ref.at[pl.ds(at if isinstance(at, int) else pl.multiple_of(at, H), H)]

    def block(ref, slot):
        at = slot * R
        return ref.at[pl.ds(at if isinstance(at, int) else pl.multiple_of(at, R), R)]

    def gx(i):
        return send(half(txt, 0, i), half(txt, 4 + 2 * x_lo + i, i), gx_s.at[i], gx_r.at[i], x_near[i])

    def g2(i):
        return send(half(txt, 6 * x_lo, 1 - i), half(txt, 4 + i, 1 - i), g2_s.at[i], g2_r.at[i], x_near[i])

    def gf(i):
        return send(half(txt, 6 - 2 * x_lo + i, i), half(txt, 1, i), gf_s.at[i], gf_r.at[i], x_near[1 - i])

    def gz(i):
        return send(half(txt, (6 + i) * (1 - x_lo), i), half(txt, 4 + i + x_lo * (2 - i), i),
                    gz_s.at[i], gz_r.at[i], z_up)

    def go(i):
        return send(block(txt, 4 * core + i), block(txt, 2 + i), go_s.at[i], go_r.at[i], other)

    def gy(i):
        return send(half(img, 0, i), half(img, 1 + i, i), gy_s.at[i], gy_r.at[i], y_near[i])

    def gw(i):
        return send(half(img, 0, 1 - i), half(img, 1 + i, 1 - i), gw_s.at[i], gw_r.at[i], y_near[i])

    def gh(i):
        return send(half(img, 1 + i, i), half(img, 3, i), gh_s.at[i], gh_r.at[i], y_near[i])

    def ids(k, src, dst, device):
        return send(src, dst, id_s.at[k], id_r.at[k], device)

    id_x = [ids(i, idt.at[0], idt.at[4 + 2 * x_lo + i], x_near[i]) for i in range(2)]
    id_f = ids(2, idt.at[6 - 2 * x_lo], idt.at[1], x_near[1])
    id_z = ids(3, idt.at[6:8], idt.at[4:6], z_up)
    id_o = ids(4, idt.at[pl.ds(4 * core, 2)], idt.at[2:4], other)
    id_y = [ids(5 + i, idi.at[0], idi.at[1 + i], y_near[i]) for i in range(2)]
    id_h = ids(7, idi.at[1], idi.at[3], y_near[0])

    loads[0].wait()
    normalize(raw_t, txt)
    loads[2].wait()
    loads[3].wait()
    pl.semaphore_wait(barrier, 6)
    for i in range(2):
        gx(i).start()

    @pl.when(low)
    def _():
        for i in range(2):
            g2(i).start()

    @pl.when(high)
    def _():
        for i in range(2):
            gz(i).start()

    loads[1].wait()
    normalize(raw_i, img)
    for i in range(2):
        gy(i).start()
    for i in range(2):
        gw(i).start()
    for copy in id_x + id_y:
        copy.start()

    @pl.when(core == 0)
    def _():
        go(0).start()

    for i in range(2):
        gx(i).wait_recv()
        gf(i).start()

        @pl.when(low)
        def _():
            gz(i).start()

    for i in range(2):
        gy(i).wait_recv()
        gh(i).start()

    @pl.when(high)
    def _():
        for i in range(2):
            gz(i).wait_recv()
            g2(1 - i).start()

    for copy in id_x + id_y:
        copy.wait_recv()
    id_f.start()
    id_h.start()

    @pl.when(low)
    def _():
        id_z.start()

    id_f.wait_recv()

    @pl.when(high | (core == 0))
    def _():
        id_o.start()

    @pl.when(high)
    def _():
        for i in range(2):
            g2(i).wait_recv()

            @pl.when(core == 1)
            def _():
                go(i).start()

    for i in range(2):
        gw(i).wait_recv()
    for i in range(2):
        gf(i).wait_recv()

    @pl.when(core == 0)
    def _():
        go(1).start()

    id_h.wait_recv()
    for s in range(4):
        keys[s * R:(s + 1) * R, :] = jnp.transpose(jnp.broadcast_to(idi[s], (128, R)))
    for i in range(2):
        gh(i).wait_recv()

    scale_value, bias_value = scale[0], bias[0]

    def pair(b):
        return pl.ds(b * 2 * R if isinstance(b, int) else pl.multiple_of(b * 2 * R, 2 * R), 2 * R)

    def weigh(b):
        for a in range(4 * R // ROWS_AT_ONCE):
            rows = slice(a * ROWS_AT_ONCE, (a + 1) * ROWS_AT_ONCE)
            dots = lax.dot_general(
                img[rows, :], txt[pair(b), :], (((1,), (1,)), ((), ())), preferred_element_type=F32)
            logits = scale_value * dots + bias_value
            mine = keys[rows, :]
            same = jnp.concatenate([mine == idt[2 * b], mine == idt[2 * b + 1]], axis=1)
            share = jax.nn.sigmoid(jnp.where(same, -logits, logits))
            weights = jnp.where(same, -share, share)
            w[rows, pair(b)] = weights.astype(BF16)
            wt[pair(b), rows] = jnp.transpose(weights).astype(BF16)

    def ro(i):
        return send(block(t_s, i), block(oc_r, i), ro_s.at[i], ro_r.at[i], other)

    def rd(i):
        return send(half(d_s, 0, i), half(d_r, 0, i), rd_s.at[i], rd_r.at[i], x_near[1 - i])

    def rc(i):
        return send(half(t_s, 2 + i, 1 - i), half(c_r, 0, 1 - i), rc_s.at[i], rc_r.at[i], x_near[i])

    def rz(i):
        return send(half(t_s, 2 + i, i), half(z_r, 0, i), rz_s.at[i], rz_r.at[i], z_down)

    def rz_on(i):
        return send(half(c_r, 0, i), half(z_r, 0, i), rz_s.at[i], rz_r.at[i], z_down)

    def rx(i):
        return send(half(x_s, 0, i), half(x_r, 0, i), rx_s.at[i], rx_r.at[i], x_near[i])

    def rh(i):
        return send(half(h_s, 0, i), half(h_r, 0, i), rh_s.at[i], rh_r.at[i], y_near[i])

    def rn(i):
        return send(half(y_s, i, 1 - i), half(y_r, i, 1 - i), rn_s.at[i], rn_r.at[i], y_near[i])

    def ra(i):
        return send(half(y_s, i, i), half(y_r, i, i), ra_s.at[i], ra_r.at[i], y_near[i])

    def text_part(b):
        return jnp.dot(wt[pair(b), :], img[...], preferred_element_type=F32)

    def image_part(a):
        return jnp.dot(w[a * 2 * R:(a + 1) * 2 * R, :], txt[0:6 * R, :], preferred_element_type=F32)

    def send_far():
        d_s[...] = gt[R:2 * R, :].astype(BF16)
        for i in range(2):
            rd(i).start()

    def send_cross():
        for i in range(2):
            rc(i).start()

        @pl.when(low)
        def _():
            for i in range(2):
                rz(i).start()

    weigh(0)
    gt[0:2 * R, :] = text_part(0)
    pl.when(core == 1)(send_far)

    @pl.when(low)
    def _():
        id_z.wait_recv()

        @pl.when(core == 1)
        def _():
            id_o.start()

        for i in range(2):
            g2(i).wait_recv()
            gz(i).wait_recv()

            @pl.when(core == 1)
            def _():
                go(i).start()

    @pl.when(core == 1)
    def _():
        id_o.wait_recv()
        for i in range(2):
            go(i).wait_recv()

    weigh(2 - core)
    t_s[pair(1 - core), :] = text_part(2 - core).astype(BF16)

    @pl.when(core == 1)
    def _():
        for i in range(2):
            ro(i).start()

    pl.when(core == 0)(send_cross)

    @pl.when(core == 0)
    def _():
        id_o.wait_recv()
        for i in range(2):
            go(i).wait_recv()

    weigh(1 + core)
    gt[2 * R:4 * R, :] = text_part(1 + core)

    @pl.when(core == 0)
    def _():
        t_s[0:2 * R, :] = gt[2 * R:4 * R, :].astype(BF16)
        for i in range(2):
            ro(i).start()

    part = image_part(1)
    h_s[...] = part[R:2 * R].astype(BF16)
    gi[2 * R:3 * R, :] = part[0:R]
    y_s[H:R, :] = part[H:R].astype(BF16)
    for i in range(2):
        rh(i).start()
    rn(0).start()

    for i in range(2):
        ro(i).wait_recv()

    @pl.when(core == 0)
    def _():
        gt[0:2 * R, :] = gt[0:2 * R, :] + oc_r[...].astype(F32)
        send_far()

    @pl.when(core == 1)
    def _():
        t_s[2 * R:4 * R, :] = (gt[2 * R:4 * R, :] + oc_r[...].astype(F32)).astype(BF16)
        send_cross()

    part = image_part(0)
    gi[0:2 * R, :] = part
    y_s[R:R + H, :] = part[R:R + H].astype(BF16)
    rn(1).start()

    for i in range(2):
        rh(i).wait_recv()
        y_s[i * R + i * H:i * R + (i + 1) * H, :] = (
            gi[(2 - i) * R + i * H:(2 - i) * R + (i + 1) * H, :] + h_r[i * H:(i + 1) * H, :].astype(F32)).astype(BF16)
        ra(i).start()

    for i in range(2):
        rc(i).wait_recv()

    @pl.when(high)
    def _():
        for i in range(2):
            rz_on(i).start()

    def send_near(i, first):
        at = slice(i * H, (i + 1) * H)
        x_s[at, :] = (first.astype(F32) + d_r[at, :].astype(F32)).astype(BF16)
        rx(i).start()

    for i in range(2):
        rd(i).wait_recv()

        @pl.when(low)
        def _():
            rz(i).wait_recv()
            send_near(i, z_r[i * H:(i + 1) * H, :])

        @pl.when(high)
        def _():
            send_near(i, t_s[(2 + i) * R + i * H:(2 + i) * R + (i + 1) * H, :])

    def backward(rows, total, out):
        values = rows[...].astype(F32)
        factor = 1.0 / jnp.sqrt(jnp.sum(values * values, axis=-1, keepdims=True) + epsilon)
        unit = values * factor
        grad = total
        along = jnp.sum(unit * grad, axis=-1, keepdims=True)
        out[...] = factor * (grad - unit * along)

    for i in range(2):
        rn(i).wait_recv()
        ra(i).wait_recv()
    backward(raw_i, gi[0:R, :] + (y_r[0:R, :].astype(F32) + y_r[R:2 * R, :].astype(F32)), image_out)

    @pl.when(high)
    def _():
        for i in range(2):
            rz(i).wait_recv()
        gt[R:2 * R, :] = gt[0:R, :] + z_r[...].astype(F32)

    @pl.when(low)
    def _():
        gt[R:2 * R, :] = gt[0:R, :] + c_r[...].astype(F32)

    for i in range(2):
        rx(i).wait_recv()
    backward(raw_t, gt[R:2 * R, :] + x_r[...].astype(F32), text_out)

    for i in range(2):
        for copy in (gx, g2, gf, gz, go, gy, gw, gh, ro, rd, rc, rz, rx, rh, rn, ra):
            copy(i).wait_send()
    for copy in id_x + id_y + [id_f, id_o, id_h]:
        copy.wait_send()

    @pl.when(low)
    def _():
        id_z.wait_send()


def shards(n_loop, images, texts, image_ids, text_ids, logit_scale, logit_bias):
    R, D = images.shape
    dma = pltpu.SemaphoreType.DMA
    vmem = pl.BlockSpec(memory_space=pltpu.VMEM)
    smem = pl.BlockSpec(memory_space=pltpu.SMEM)
    anywhere = pl.BlockSpec(memory_space=pltpu.HBM)

    def rows(count, dtype=BF16):
        return pltpu.VMEM((count * R, D), dtype)

    image_rows, text_rows = pl.pallas_call(
        functools.partial(kernel, n_loop),
        out_shape=(jax.ShapeDtypeStruct((R, D), F32), jax.ShapeDtypeStruct((R, D), F32)),
        in_specs=[anywhere, anywhere, anywhere, anywhere, smem, smem],
        out_specs=(vmem, vmem),
        scratch_shapes=[
            rows(1), rows(1), rows(4), rows(8),
            pltpu.VMEM((4, 1, R), jnp.int32), pltpu.VMEM((8, 1, R), jnp.int32), pltpu.VMEM((4 * R, 128), jnp.int32),
            pltpu.VMEM((4 * R, 6 * R), BF16), pltpu.VMEM((6 * R, 4 * R), BF16), rows(4, F32), rows(3, F32),
            rows(4), rows(2), rows(1), rows(1), rows(1), rows(1), rows(1), rows(1), rows(1), rows(1),
            rows(2), rows(2), dma((4,)),
        ] + [dma((2,))] * 16 + [dma((8,))] * 2 + [dma((2,))] * 16,
        compiler_params=pltpu.CompilerParams(
            collective_id=0, has_side_effects=True, vmem_limit_bytes=56 * 1024 * 1024),
        cost_estimate=pl.CostEstimate(
            flops=6 * 4 * R * 6 * R * D, bytes_accessed=12 * R * D, transcendentals=24 * R * R),
    )(images, texts, image_ids.reshape(1, R), text_ids.reshape(1, R), logit_scale, logit_bias)
    return image_rows * logit_scale[0], text_rows * logit_scale[0]


def solution(mesh):
    rows = P(("loop", "group"), None)
    ids = P(("loop", "group"))
    return jax.shard_map(
        functools.partial(shards, mesh.shape["loop"]), mesh=mesh,
        in_specs=(rows, rows, ids, ids, P(), P()), out_specs=(rows, rows), check_vma=False)
```

```python
import functools

import jax
import jax.numpy as jnp
from jax import lax
from jax.experimental import pallas as pl
from jax.experimental.pallas import tpu as pltpu
from jax.sharding import PartitionSpec as P

epsilon = 1e-06
MESH = pl.DeviceIdType.MESH
F32, BF16 = jnp.float32, jnp.bfloat16
ROWS_AT_ONCE = 256
PIECES = 2
PARTS = 2


def kernel(
    n_loop, images, texts, image_ids, text_ids, scale, bias, image_out, text_out,
    raw_i, raw_t, img, txt, idi, idt, keys, w, wt, gt, gi,
    t_s, oc_r, d_s, d_r, c_r, z_r, x_s, x_r, h_s, h_r, y_s, y_r,
    load, gx_s, gx_r, g2_s, g2_r, gf_s, gf_r, gz_s, gz_r, go_s, go_r, gy_s, gy_r, gw_s, gw_r, gh_s, gh_r, id_s, id_r,
    ro_s, ro_r, rd_s, rd_r, rc_s, rc_r, rz_s, rz_r, rx_s, rx_r, rh_s, rh_r, rn_s, rn_r, ra_s, ra_r,
):
    R, D = raw_i.shape
    H = R // 2
    loop, group = lax.axis_index("loop"), lax.axis_index("group")
    core = lax.rem(loop, 2)
    x_lo = lax.rem(loop // 2, 2)
    y, x_hi = group // 2, lax.rem(group, 2)
    flip = loop + 2 - 4 * x_lo
    other = (loop + 1 - 2 * core, group)
    x_near = ((flip, group), (flip, group + 1 - 2 * x_hi))
    y_near = ((loop, lax.rem(y + 1, 4) * 2 + x_hi), (loop, lax.rem(y + 3, 4) * 2 + x_hi))
    z_up = (lax.rem(loop + 4, n_loop), group)
    z_down = (lax.rem(loop + n_loop - 4, n_loop), group)
    low, high = x_lo == 0, x_lo == 1

    loads = [
        pltpu.make_async_copy(src, dst, load.at[i])
        for i, (src, dst) in enumerate(
            [(texts, raw_t), (images, raw_i), (text_ids, idt.at[0]), (image_ids, idi.at[0])])
    ]
    for copy in loads:
        copy.start()
    barrier = pltpu.get_barrier_semaphore()
    for device in (*x_near, *y_near, z_down, other):
        pl.semaphore_signal(barrier, inc=1, device_id=device, device_id_type=MESH)

    def normalize(rows, block):
        values = rows[...].astype(F32)
        factor = 1.0 / jnp.sqrt(jnp.sum(values * values, axis=-1, keepdims=True) + epsilon)
        block[0:R, :] = (values * factor).astype(BF16)

    def send(src, dst, s, r, device):
        return pltpu.make_async_remote_copy(
            src_ref=src, dst_ref=dst, send_sem=s, recv_sem=r, device_id=device, device_id_type=MESH)

    def half(ref, slot, h, q, count):
        size = H // count
        at = slot * R + h * H + q * size
        return ref.at[pl.ds(at if isinstance(at, int) else pl.multiple_of(at, size), size)]

    def block(ref, slot):
        at = slot * R
        return ref.at[pl.ds(at if isinstance(at, int) else pl.multiple_of(at, R), R)]

    def gx(i, q):
        return send(half(txt, 0, i, q, PIECES), half(txt, 4 + 2 * x_lo + i, i, q, PIECES), gx_s.at[i, q], gx_r.at[i, q], x_near[i])

    def g2(i, q):
        return send(half(txt, 6 * x_lo, 1 - i, q, PIECES), half(txt, 4 + i, 1 - i, q, PIECES), g2_s.at[i, q], g2_r.at[i, q], x_near[i])

    def gf(i, q):
        return send(half(txt, 6 - 2 * x_lo + i, i, q, PIECES), half(txt, 1, i, q, PIECES), gf_s.at[i, q], gf_r.at[i, q], x_near[1 - i])

    def gz(i, q):
        return send(half(txt, (6 + i) * (1 - x_lo), i, q, PIECES), half(txt, 4 + i + x_lo * (2 - i), i, q, PIECES),
                    gz_s.at[i, q], gz_r.at[i, q], z_up)

    def go(i, h):
        return send(half(txt, 4 * core + i, h, 0, 1), half(txt, 2 + i, h, 0, 1), go_s.at[i, h], go_r.at[i, h], other)

    def gy(i, q):
        return send(half(img, 0, i, q, PIECES), half(img, 1 + i, i, q, PIECES), gy_s.at[i, q], gy_r.at[i, q], y_near[i])

    def gw(i, q):
        return send(half(img, 0, 1 - i, q, PIECES), half(img, 1 + i, 1 - i, q, PIECES), gw_s.at[i, q], gw_r.at[i, q], y_near[i])

    def gh(i, q):
        return send(half(img, 1 + i, i, q, PIECES), half(img, 3, i, q, PIECES), gh_s.at[i, q], gh_r.at[i, q], y_near[i])

    def ids(k, src, dst, device):
        return send(src, dst, id_s.at[k], id_r.at[k], device)

    id_x = [ids(i, idt.at[0], idt.at[4 + 2 * x_lo + i], x_near[i]) for i in range(2)]
    id_f = ids(2, idt.at[6 - 2 * x_lo], idt.at[1], x_near[1])
    id_z = ids(3, idt.at[6:8], idt.at[4:6], z_up)
    id_o = ids(4, idt.at[pl.ds(4 * core, 2)], idt.at[2:4], other)
    id_y = [ids(5 + i, idi.at[0], idi.at[1 + i], y_near[i]) for i in range(2)]
    id_h = ids(7, idi.at[1], idi.at[3], y_near[0])

    def pieces(count):
        return [(i, q) for q in range(count) for i in range(2)]

    loads[0].wait()
    normalize(raw_t, txt)
    loads[2].wait()
    loads[3].wait()
    pl.semaphore_wait(barrier, 6)
    for copy in id_x + id_y:
        copy.start()
    for i, q in pieces(PIECES):
        gx(i, q).start()

    @pl.when(low)
    def _():
        for i, q in pieces(PIECES):
            g2(i, q).start()

    @pl.when(high)
    def _():
        for i, q in pieces(PIECES):
            gz(i, q).start()

    loads[1].wait()
    normalize(raw_i, img)
    for i, q in pieces(PIECES):
        gy(i, q).start()
    for i, q in pieces(PIECES):
        gw(i, q).start()

    @pl.when(core == 0)
    def _():
        for h in range(2):
            go(0, h).start()

    for copy in id_x + id_y:
        copy.wait_recv()
    id_f.start()
    id_h.start()

    @pl.when(low)
    def _():
        id_z.start()

    for q in range(PIECES):
        for i in range(2):
            gx(i, q).wait_recv()
            gf(i, q).start()

            @pl.when(low)
            def _():
                gz(i, q).start()

        for i in range(2):
            gy(i, q).wait_recv()
            gh(i, q).start()

    def pass_sideways(q):
        for i in range(2):
            gz(i, q).wait_recv()
            g2(1 - i, q).start()

    pl.when(high)(lambda: pass_sideways(0))
    pl.when(high & (loop >= 4))(lambda: pass_sideways(1))
    id_f.wait_recv()

    @pl.when(high | (core == 0))
    def _():
        id_o.start()

    @pl.when(high)
    def _():
        for i in range(2):
            for q in range(PIECES):
                g2(i, q).wait_recv()

            @pl.when(core == 1)
            def _():
                for h in range(2):
                    go(i, h).start()

    for i, q in pieces(PIECES):
        gw(i, q).wait_recv()
    for i in range(2):
        for q in range(PIECES):
            gf(i, q).wait_recv()

        @pl.when(core == 0)
        def _():
            go(1, i).start()

    id_h.wait_recv()
    for s in range(4):
        keys[s * R:(s + 1) * R, :] = jnp.transpose(jnp.broadcast_to(idi[s], (128, R)))
    for i, q in pieces(PIECES):
        gh(i, q).wait_recv()

    scale_value, bias_value = scale[0], bias[0]

    def pair(b):
        return pl.ds(b * 2 * R if isinstance(b, int) else pl.multiple_of(b * 2 * R, 2 * R), 2 * R)

    def weigh(b):
        for a in range(4 * R // ROWS_AT_ONCE):
            rows = slice(a * ROWS_AT_ONCE, (a + 1) * ROWS_AT_ONCE)
            dots = lax.dot_general(
                img[rows, :], txt[pair(b), :], (((1,), (1,)), ((), ())), preferred_element_type=F32)
            logits = scale_value * dots + bias_value
            mine = keys[rows, :]
            same = jnp.concatenate([mine == idt[2 * b], mine == idt[2 * b + 1]], axis=1)
            share = jax.nn.sigmoid(jnp.where(same, -logits, logits))
            weights = jnp.where(same, -share, share)
            w[rows, pair(b)] = weights.astype(BF16)
            wt[pair(b), rows] = jnp.transpose(weights).astype(BF16)

    def ro(i):
        return send(block(t_s, i), block(oc_r, i), ro_s.at[i], ro_r.at[i], other)

    def rd(i, q):
        return send(half(d_s, 0, i, q, PARTS), half(d_r, 0, i, q, PARTS), rd_s.at[i, q], rd_r.at[i, q], x_near[1 - i])

    def rc(i, q):
        return send(half(t_s, 2 + i, 1 - i, q, PARTS), half(c_r, 0, 1 - i, q, PARTS), rc_s.at[i, q], rc_r.at[i, q], x_near[i])

    def rz(i, q):
        return send(half(t_s, 2 + i, i, q, PARTS), half(z_r, 0, i, q, PARTS), rz_s.at[i, q], rz_r.at[i, q], z_down)

    def rz_on(i, q):
        return send(half(c_r, 0, i, q, PARTS), half(z_r, 0, i, q, PARTS), rz_s.at[i, q], rz_r.at[i, q], z_down)

    def rx(i, q):
        return send(half(x_s, 0, i, q, PARTS), half(x_r, 0, i, q, PARTS), rx_s.at[i, q], rx_r.at[i, q], x_near[i])

    def rh(i, q):
        return send(half(h_s, 0, i, q, PARTS), half(h_r, 0, i, q, PARTS), rh_s.at[i, q], rh_r.at[i, q], y_near[i])

    def rn(i, q):
        return send(half(y_s, i, 1 - i, q, PARTS), half(y_r, i, 1 - i, q, PARTS), rn_s.at[i, q], rn_r.at[i, q], y_near[i])

    def ra(i, q):
        return send(half(y_s, i, i, q, PARTS), half(y_r, i, i, q, PARTS), ra_s.at[i, q], ra_r.at[i, q], y_near[i])

    def text_part(b):
        return jnp.dot(wt[pair(b), :], img[...], preferred_element_type=F32)

    def image_part(a):
        return jnp.dot(w[a * 2 * R:(a + 1) * 2 * R, :], txt[0:6 * R, :], preferred_element_type=F32)

    def send_far():
        d_s[...] = gt[R:2 * R, :].astype(BF16)
        for i, q in pieces(PARTS):
            rd(i, q).start()

    def send_cross():
        for i, q in pieces(PARTS):
            rc(i, q).start()

        @pl.when(low)
        def _():
            for i, q in pieces(PARTS):
                rz(i, q).start()

    weigh(0)
    gt[0:2 * R, :] = text_part(0)
    pl.when(core == 1)(send_far)
    pl.when(high & (loop < 4))(lambda: pass_sideways(1))

    def from_below():
        id_z.wait_recv()

        @pl.when(core == 1)
        def _():
            id_o.start()

        for i in range(2):
            for q in range(PIECES):
                gz(i, q).wait_recv()

            @pl.when(core == 1)
            def _():
                go(i, i).start()

        for i in range(2):
            for q in range(PIECES):
                g2(i, q).wait_recv()

            @pl.when(core == 1)
            def _():
                go(i, 1 - i).start()

    def from_other():
        id_o.wait_recv()
        for i in range(2):
            for h in range(2):
                go(i, h).wait_recv()

    def image_far():
        part = image_part(1)
        h_s[...] = part[R:2 * R].astype(BF16)
        gi[2 * R:3 * R, :] = part[0:R]
        y_s[H:R, :] = part[H:R].astype(BF16)
        for i, q in pieces(PARTS):
            rh(i, q).start()
        for q in range(PARTS):
            rn(0, q).start()

    def image_near():
        part = image_part(0)
        gi[0:2 * R, :] = part
        y_s[R:R + H, :] = part[R:R + H].astype(BF16)
        for q in range(PARTS):
            rn(1, q).start()

    pl.when(low)(from_below)
    pl.when(core == 1)(from_other)
    weigh(2 - core)
    t_s[pair(1 - core), :] = text_part(2 - core).astype(BF16)

    @pl.when(core == 1)
    def _():
        for i in range(2):
            ro(i).start()

    pl.when(core == 0)(send_cross)

    pl.when(core == 0)(from_other)
    weigh(1 + core)

    @pl.when(core == 0)
    def _():
        for i in range(2):
            ro(i).wait_recv()
        gt[0:2 * R, :] = gt[0:2 * R, :] + oc_r[...].astype(F32)
        send_far()


    gt[2 * R:4 * R, :] = text_part(1 + core)

    @pl.when(core == 0)
    def _():
        t_s[0:2 * R, :] = gt[2 * R:4 * R, :].astype(BF16)
        for i in range(2):
            ro(i).start()

    image_far()
    @pl.when(core == 1)
    def _():
        for i in range(2):
            ro(i).wait_recv()
        t_s[2 * R:4 * R, :] = (gt[2 * R:4 * R, :] + oc_r[...].astype(F32)).astype(BF16)
        send_cross()

    image_near()


    def piece(h, q):
        return slice(h * H + q * (H // PARTS), h * H + (q + 1) * (H // PARTS))

    def shifted(at, slot):
        return slice(slot * R + at.start, slot * R + at.stop)

    for i, q in pieces(PARTS):
        rh(i, q).wait_recv()
        at = piece(i, q)
        y_s[shifted(at, i), :] = (gi[shifted(at, 2 - i), :] + h_r[at, :].astype(F32)).astype(BF16)
        ra(i, q).start()

    @pl.when(high)
    def _():
        for i, q in pieces(PARTS):
            rc(i, q).wait_recv()
            rz_on(1 - i, q).start()

    def send_near(i, q, first):
        at = piece(i, q)
        x_s[at, :] = (first.astype(F32) + d_r[at, :].astype(F32)).astype(BF16)
        rx(i, q).start()

    for i, q in pieces(PARTS):
        rd(i, q).wait_recv()

        @pl.when(low)
        def _():
            rz(i, q).wait_recv()
            send_near(i, q, z_r[piece(i, q), :])

        @pl.when(high)
        def _():
            send_near(i, q, t_s[shifted(piece(i, q), 2 + i), :])

    def backward(rows, total, out):
        values = rows[...].astype(F32)
        factor = 1.0 / jnp.sqrt(jnp.sum(values * values, axis=-1, keepdims=True) + epsilon)
        unit = values * factor
        grad = total
        along = jnp.sum(unit * grad, axis=-1, keepdims=True)
        out[...] = factor * (grad - unit * along)

    for i, q in pieces(PARTS):
        rn(i, q).wait_recv()
        ra(i, q).wait_recv()
    backward(raw_i, gi[0:R, :] + (y_r[0:R, :].astype(F32) + y_r[R:2 * R, :].astype(F32)), image_out)

    @pl.when(high)
    def _():
        for i, q in pieces(PARTS):
            rz(i, q).wait_recv()
        gt[R:2 * R, :] = gt[0:R, :] + z_r[...].astype(F32)

    @pl.when(low)
    def _():
        for i, q in pieces(PARTS):
            rc(i, q).wait_recv()
        gt[R:2 * R, :] = gt[0:R, :] + c_r[...].astype(F32)

    for i, q in pieces(PARTS):
        rx(i, q).wait_recv()
    backward(raw_t, gt[R:2 * R, :] + x_r[...].astype(F32), text_out)

    for copy in (gx, g2, gf, gz, gy, gw, gh):
        for i, q in pieces(PIECES):
            copy(i, q).wait_send()
    for copy in (rd, rc, rz, rx, rh, rn, ra):
        for i, q in pieces(PARTS):
            copy(i, q).wait_send()
    for i in range(2):
        for h in range(2):
            go(i, h).wait_send()
        ro(i).wait_send()
    for copy in id_x + id_y + [id_f, id_o, id_h]:
        copy.wait_send()

    @pl.when(low)
    def _():
        id_z.wait_send()


def shards(n_loop, images, texts, image_ids, text_ids, logit_scale, logit_bias):
    R, D = images.shape
    dma = pltpu.SemaphoreType.DMA
    vmem = pl.BlockSpec(memory_space=pltpu.VMEM)
    smem = pl.BlockSpec(memory_space=pltpu.SMEM)
    anywhere = pl.BlockSpec(memory_space=pltpu.HBM)

    def rows(count, dtype=BF16):
        return pltpu.VMEM((count * R, D), dtype)

    image_rows, text_rows = pl.pallas_call(
        functools.partial(kernel, n_loop),
        out_shape=(pltpu.VMEM((R, D), F32), pltpu.VMEM((R, D), F32)),
        in_specs=[anywhere, anywhere, anywhere, anywhere, smem, smem],
        out_specs=(vmem, vmem),
        scratch_shapes=[
            rows(1), rows(1), rows(4), rows(8),
            pltpu.VMEM((4, 1, R), jnp.int32), pltpu.VMEM((8, 1, R), jnp.int32), pltpu.VMEM((4 * R, 128), jnp.int32),
            pltpu.VMEM((4 * R, 6 * R), BF16), pltpu.VMEM((6 * R, 4 * R), BF16), rows(4, F32), rows(3, F32),
            rows(4), rows(2), rows(1), rows(1), rows(1), rows(1), rows(1), rows(1), rows(1), rows(1),
            rows(2), rows(2), dma((4,)),
        ] + [dma((2, PIECES))] * 8 + [dma((2, 2))] * 2 + [dma((2, PIECES))] * 6 + [dma((8,))] * 2
        + [dma((2,))] * 2 + [dma((2, PARTS))] * 14,
        compiler_params=pltpu.CompilerParams(
            collective_id=0, has_side_effects=True, vmem_limit_bytes=24 * 1024 * 1024),
        cost_estimate=pl.CostEstimate(
            flops=6 * 4 * R * 6 * R * D, bytes_accessed=12 * R * D, transcendentals=24 * R * R),
    )(*[pltpu.with_memory_space_constraint(x, pltpu.HBM)
        for x in (images, texts, image_ids.reshape(1, R), text_ids.reshape(1, R))], logit_scale, logit_bias)
    return image_rows * logit_scale[0], text_rows * logit_scale[0]


def solution(mesh):
    rows = P(("loop", "group"), None)
    ids = P(("loop", "group"))
    return jax.shard_map(
        functools.partial(shards, mesh.shape["loop"]), mesh=mesh,
        in_specs=(rows, rows, ids, ids, P(), P()), out_specs=(rows, rows), check_vma=False)
```

```python
import functools

import jax
import jax.numpy as jnp
from jax import lax
from jax.experimental import pallas as pl
from jax.experimental.pallas import tpu as pltpu
from jax.sharding import PartitionSpec as P

epsilon = 1e-06
MESH = pl.DeviceIdType.MESH
F32, BF16 = jnp.float32, jnp.bfloat16
ROWS_AT_ONCE = 256
PIECES = 2
PARTS = 2


def kernel(
    n_loop, images, texts, image_ids, text_ids, scale, bias, image_out, text_out,
    raw_i, raw_t, img, txt, idi, idt, keys, w, wt, gt, gi,
    t_s, oc_r, d_s, d_r, c_r, z_r, x_s, x_r, h_s, h_r, y_s, y_r,
    load, gx_s, gx_r, g2_s, g2_r, gf_s, gf_r, gz_s, gz_r, go_s, go_r, gy_s, gy_r, gw_s, gw_r, gh_s, gh_r, id_s, id_r,
    ro_s, ro_r, rd_s, rd_r, rc_s, rc_r, rz_s, rz_r, rx_s, rx_r, rh_s, rh_r, rn_s, rn_r, ra_s, ra_r,
):
    R, D = raw_i.shape
    H = R // 2
    loop, group = lax.axis_index("loop"), lax.axis_index("group")
    core = lax.rem(loop, 2)
    x_lo = lax.rem(loop // 2, 2)
    y, x_hi = group // 2, lax.rem(group, 2)
    flip = loop + 2 - 4 * x_lo
    other = (loop + 1 - 2 * core, group)
    x_near = ((flip, group), (flip, group + 1 - 2 * x_hi))
    y_near = ((loop, lax.rem(y + 1, 4) * 2 + x_hi), (loop, lax.rem(y + 3, 4) * 2 + x_hi))
    z_up = (lax.rem(loop + 4, n_loop), group)
    z_down = (lax.rem(loop + n_loop - 4, n_loop), group)
    low, high = x_lo == 0, x_lo == 1

    loads = [
        pltpu.make_async_copy(src, dst, load.at[i])
        for i, (src, dst) in enumerate(
            [(texts, raw_t), (images, raw_i), (text_ids, idt.at[0]), (image_ids, idi.at[0])])
    ]
    for copy in loads:
        copy.start()
    barrier = pltpu.get_barrier_semaphore()
    for device in (*x_near, *y_near, z_down, other):
        pl.semaphore_signal(barrier, inc=1, device_id=device, device_id_type=MESH)

    def normalize(rows, block):
        values = rows[...].astype(F32)
        factor = 1.0 / jnp.sqrt(jnp.sum(values * values, axis=-1, keepdims=True) + epsilon)
        block[0:R, :] = (values * factor).astype(BF16)

    def send(src, dst, s, r, device):
        return pltpu.make_async_remote_copy(
            src_ref=src, dst_ref=dst, send_sem=s, recv_sem=r, device_id=device, device_id_type=MESH)

    def half(ref, slot, h, q, count):
        size = H // count
        at = slot * R + h * H + q * size
        return ref.at[pl.ds(at if isinstance(at, int) else pl.multiple_of(at, size), size)]

    def block(ref, slot):
        at = slot * R
        return ref.at[pl.ds(at if isinstance(at, int) else pl.multiple_of(at, R), R)]

    def gx(i, q):
        return send(half(txt, 0, i, q, PIECES), half(txt, 4 + 2 * x_lo + i, i, q, PIECES), gx_s.at[i, q], gx_r.at[i, q], x_near[i])

    def g2(i, q):
        return send(half(txt, 6 * x_lo, 1 - i, q, PIECES), half(txt, 4 + i, 1 - i, q, PIECES), g2_s.at[i, q], g2_r.at[i, q], x_near[i])

    def gf(i, q):
        return send(half(txt, 6 - 2 * x_lo + i, i, q, PIECES), half(txt, 1, i, q, PIECES), gf_s.at[i, q], gf_r.at[i, q], x_near[1 - i])

    def gz(i, q):
        return send(half(txt, (6 + i) * (1 - x_lo), i, q, PIECES), half(txt, 4 + i + x_lo * (2 - i), i, q, PIECES),
                    gz_s.at[i, q], gz_r.at[i, q], z_up)

    def go(i, h):
        return send(half(txt, 4 * core + i, h, 0, 1), half(txt, 2 + i, h, 0, 1), go_s.at[i, h], go_r.at[i, h], other)

    def gy(i, q):
        return send(half(img, 0, i, q, PIECES), half(img, 1 + i, i, q, PIECES), gy_s.at[i, q], gy_r.at[i, q], y_near[i])

    def gw(i, q):
        return send(half(img, 0, 1 - i, q, PIECES), half(img, 1 + i, 1 - i, q, PIECES), gw_s.at[i, q], gw_r.at[i, q], y_near[i])

    def gh(i, q):
        return send(half(img, 1 + i, i, q, PIECES), half(img, 3, i, q, PIECES), gh_s.at[i, q], gh_r.at[i, q], y_near[i])

    def ids(k, src, dst, device):
        return send(src, dst, id_s.at[k], id_r.at[k], device)

    id_x = [ids(i, idt.at[0], idt.at[4 + 2 * x_lo + i], x_near[i]) for i in range(2)]
    id_f = ids(2, idt.at[6 - 2 * x_lo], idt.at[1], x_near[1])
    id_z = ids(3, idt.at[6:8], idt.at[4:6], z_up)
    id_o = ids(4, idt.at[pl.ds(4 * core, 2)], idt.at[2:4], other)
    id_y = [ids(5 + i, idi.at[0], idi.at[1 + i], y_near[i]) for i in range(2)]
    id_h = ids(7, idi.at[1], idi.at[3], y_near[0])

    def pieces(count):
        return [(i, q) for q in range(count) for i in range(2)]

    loads[0].wait()
    normalize(raw_t, txt)
    loads[2].wait()
    loads[3].wait()
    pl.semaphore_wait(barrier, 6)
    for copy in id_x + id_y:
        copy.start()
    for i, q in pieces(PIECES):
        gx(i, q).start()

    @pl.when(low)
    def _():
        for i, q in pieces(PIECES):
            g2(i, q).start()

    @pl.when(high)
    def _():
        for i, q in pieces(PIECES):
            gz(i, q).start()

    loads[1].wait()
    normalize(raw_i, img)
    for i, q in pieces(PIECES):
        gy(i, q).start()
    for i, q in pieces(PIECES):
        gw(i, q).start()

    @pl.when(core == 0)
    def _():
        for h in range(2):
            go(0, h).start()

    for copy in id_x + id_y:
        copy.wait_recv()
    id_f.start()
    id_h.start()

    @pl.when(low)
    def _():
        id_z.start()

    for q in range(PIECES):
        for i in range(2):
            gx(i, q).wait_recv()
            gf(i, q).start()

            @pl.when(low)
            def _():
                gz(i, q).start()

        for i in range(2):
            gy(i, q).wait_recv()
            gh(i, q).start()

    def pass_sideways(q):
        for i in range(2):
            gz(i, q).wait_recv()
            g2(1 - i, q).start()

    pl.when(high)(lambda: pass_sideways(0))
    pl.when(high & (loop >= 4))(lambda: pass_sideways(1))
    id_f.wait_recv()

    @pl.when(high | (core == 0))
    def _():
        id_o.start()

    @pl.when(high)
    def _():
        for i in range(2):
            for q in range(PIECES):
                g2(i, q).wait_recv()

            @pl.when(core == 1)
            def _():
                for h in range(2):
                    go(i, h).start()

    for i, q in pieces(PIECES):
        gw(i, q).wait_recv()
    for i in range(2):
        for q in range(PIECES):
            gf(i, q).wait_recv()

        @pl.when(core == 0)
        def _():
            go(1, i).start()

    id_h.wait_recv()
    for s in range(4):
        keys[s * R:(s + 1) * R, :] = jnp.transpose(jnp.broadcast_to(idi[s], (128, R)))
    for i, q in pieces(PIECES):
        gh(i, q).wait_recv()

    scale_value, bias_value = scale[0], bias[0]

    def pair(b):
        return pl.ds(b * 2 * R if isinstance(b, int) else pl.multiple_of(b * 2 * R, 2 * R), 2 * R)

    def weigh(b):
        for a in range(4 * R // ROWS_AT_ONCE):
            rows = slice(a * ROWS_AT_ONCE, (a + 1) * ROWS_AT_ONCE)
            dots = lax.dot_general(
                img[rows, :], txt[pair(b), :], (((1,), (1,)), ((), ())), preferred_element_type=F32)
            logits = scale_value * dots + bias_value
            mine = keys[rows, :]
            same = jnp.concatenate([mine == idt[2 * b], mine == idt[2 * b + 1]], axis=1)
            share = jax.nn.sigmoid(jnp.where(same, -logits, logits))
            weights = jnp.where(same, -share, share)
            w[rows, pair(b)] = weights.astype(BF16)
            wt[pair(b), rows] = jnp.transpose(weights).astype(BF16)

    def ro(i):
        return send(block(t_s, i), block(oc_r, i), ro_s.at[i], ro_r.at[i], other)

    def rd(i, q):
        return send(half(d_s, 0, i, q, PARTS), half(d_r, 0, i, q, PARTS), rd_s.at[i, q], rd_r.at[i, q], x_near[1 - i])

    def rc(i, q):
        return send(half(t_s, 2 + i, 1 - i, q, PARTS), half(c_r, 0, 1 - i, q, PARTS), rc_s.at[i, q], rc_r.at[i, q], x_near[i])

    def rz(i, q):
        return send(half(t_s, 2 + i, i, q, PARTS), half(z_r, 0, i, q, PARTS), rz_s.at[i, q], rz_r.at[i, q], z_down)

    def rz_on(i, q):
        return send(half(c_r, 0, i, q, PARTS), half(z_r, 0, i, q, PARTS), rz_s.at[i, q], rz_r.at[i, q], z_down)

    def rx(i, q):
        return send(half(x_s, 0, i, q, PARTS), half(x_r, 0, i, q, PARTS), rx_s.at[i, q], rx_r.at[i, q], x_near[i])

    def rh(i, q):
        return send(half(h_s, 0, i, q, PARTS), half(h_r, 0, i, q, PARTS), rh_s.at[i, q], rh_r.at[i, q], y_near[i])

    def rn(i, q):
        return send(half(y_s, i, 1 - i, q, PARTS), half(y_r, i, 1 - i, q, PARTS), rn_s.at[i, q], rn_r.at[i, q], y_near[i])

    def ra(i, q):
        return send(half(y_s, i, i, q, PARTS), half(y_r, i, i, q, PARTS), ra_s.at[i, q], ra_r.at[i, q], y_near[i])

    def text_part(b):
        return jnp.dot(wt[pair(b), :], img[...], preferred_element_type=F32)

    def image_part(a):
        return jnp.dot(w[a * 2 * R:(a + 1) * 2 * R, :], txt[0:6 * R, :], preferred_element_type=F32)

    def send_far():
        d_s[...] = gt[R:2 * R, :].astype(BF16)
        for i, q in pieces(PARTS):
            rd(i, q).start()

    def send_cross():
        for i, q in pieces(PARTS):
            rc(i, q).start()

        @pl.when(low)
        def _():
            for i, q in pieces(PARTS):
                rz(i, q).start()

    def from_below():
        id_z.wait_recv()

        @pl.when(core == 1)
        def _():
            id_o.start()

        for i in range(2):
            for q in range(PIECES):
                gz(i, q).wait_recv()

            @pl.when(core == 1)
            def _():
                go(i, i).start()

        for i in range(2):
            for q in range(PIECES):
                g2(i, q).wait_recv()

            @pl.when(core == 1)
            def _():
                go(i, 1 - i).start()

    def from_other():
        id_o.wait_recv()
        for i in range(2):
            for h in range(2):
                go(i, h).wait_recv()

    def image_far():
        part = image_part(1)
        h_s[...] = part[R:2 * R].astype(BF16)
        gi[2 * R:3 * R, :] = part[0:R]
        y_s[H:R, :] = part[H:R].astype(BF16)
        for i, q in pieces(PARTS):
            rh(i, q).start()
        for q in range(PARTS):
            rn(0, q).start()

    def image_near():
        part = image_part(0)
        gi[0:2 * R, :] = part
        y_s[R:R + H, :] = part[R:R + H].astype(BF16)
        for q in range(PARTS):
            rn(1, q).start()

    weigh(0)
    gt[0:2 * R, :] = text_part(0)
    pl.when(core == 1)(send_far)
    pl.when(high & (loop < 4))(lambda: pass_sideways(1))
    pl.when(low)(from_below)
    pl.when(core == 1)(from_other)
    weigh(2 - core)
    t_s[pair(1 - core), :] = text_part(2 - core).astype(BF16)

    @pl.when(core == 1)
    def _():
        for i in range(2):
            ro(i).start()

    pl.when(core == 0)(send_cross)
    pl.when(core == 0)(from_other)
    weigh(1 + core)
    image_far()

    @pl.when(core == 0)
    def _():
        for i in range(2):
            ro(i).wait_recv()
        gt[0:2 * R, :] = gt[0:2 * R, :] + oc_r[...].astype(F32)
        send_far()

    gt[2 * R:4 * R, :] = text_part(1 + core)

    @pl.when(core == 0)
    def _():
        t_s[0:2 * R, :] = gt[2 * R:4 * R, :].astype(BF16)
        for i in range(2):
            ro(i).start()


    @pl.when(core == 1)
    def _():
        for i in range(2):
            ro(i).wait_recv()
        t_s[2 * R:4 * R, :] = (gt[2 * R:4 * R, :] + oc_r[...].astype(F32)).astype(BF16)
        send_cross()

    image_near()

    def piece(h, q):
        return slice(h * H + q * (H // PARTS), h * H + (q + 1) * (H // PARTS))

    def shifted(at, slot):
        return slice(slot * R + at.start, slot * R + at.stop)

    @pl.when(high)
    def _():
        for i, q in pieces(PARTS):
            rc(i, q).wait_recv()
            rz_on(1 - i, q).start()

    for i, q in pieces(PARTS):
        rh(i, q).wait_recv()
        at = piece(i, q)
        y_s[shifted(at, i), :] = (gi[shifted(at, 2 - i), :] + h_r[at, :].astype(F32)).astype(BF16)
        ra(i, q).start()

    def send_near(i, q, first):
        at = piece(i, q)
        x_s[at, :] = (first.astype(F32) + d_r[at, :].astype(F32)).astype(BF16)
        rx(i, q).start()

    for i, q in pieces(PARTS):
        rd(i, q).wait_recv()

        @pl.when(low)
        def _():
            rz(i, q).wait_recv()
            send_near(i, q, z_r[piece(i, q), :])

        @pl.when(high)
        def _():
            send_near(i, q, t_s[shifted(piece(i, q), 2 + i), :])

    def backward(rows, total, out):
        values = rows[...].astype(F32)
        factor = 1.0 / jnp.sqrt(jnp.sum(values * values, axis=-1, keepdims=True) + epsilon)
        unit = values * factor
        grad = total
        along = jnp.sum(unit * grad, axis=-1, keepdims=True)
        out[...] = factor * (grad - unit * along)

    for i, q in pieces(PARTS):
        rn(i, q).wait_recv()
        ra(i, q).wait_recv()
    backward(raw_i, gi[0:R, :] + (y_r[0:R, :].astype(F32) + y_r[R:2 * R, :].astype(F32)), image_out)

    @pl.when(high)
    def _():
        for i, q in pieces(PARTS):
            rz(i, q).wait_recv()
        gt[R:2 * R, :] = gt[0:R, :] + z_r[...].astype(F32)

    @pl.when(low)
    def _():
        for i, q in pieces(PARTS):
            rc(i, q).wait_recv()
        gt[R:2 * R, :] = gt[0:R, :] + c_r[...].astype(F32)

    for i, q in pieces(PARTS):
        rx(i, q).wait_recv()
    backward(raw_t, gt[R:2 * R, :] + x_r[...].astype(F32), text_out)

    for copy in (gx, g2, gf, gz, gy, gw, gh):
        for i, q in pieces(PIECES):
            copy(i, q).wait_send()
    for copy in (rd, rc, rz, rx, rh, rn, ra):
        for i, q in pieces(PARTS):
            copy(i, q).wait_send()
    for i in range(2):
        for h in range(2):
            go(i, h).wait_send()
        ro(i).wait_send()
    for copy in id_x + id_y + [id_f, id_o, id_h]:
        copy.wait_send()

    @pl.when(low)
    def _():
        id_z.wait_send()


def shards(n_loop, images, texts, image_ids, text_ids, logit_scale, logit_bias):
    R, D = images.shape
    dma = pltpu.SemaphoreType.DMA
    vmem = pl.BlockSpec(memory_space=pltpu.VMEM)
    smem = pl.BlockSpec(memory_space=pltpu.SMEM)
    anywhere = pl.BlockSpec(memory_space=pltpu.HBM)

    def rows(count, dtype=BF16):
        return pltpu.VMEM((count * R, D), dtype)

    image_rows, text_rows = pl.pallas_call(
        functools.partial(kernel, n_loop),
        out_shape=(pltpu.VMEM((R, D), F32), pltpu.VMEM((R, D), F32)),
        in_specs=[anywhere, anywhere, anywhere, anywhere, smem, smem],
        out_specs=(vmem, vmem),
        scratch_shapes=[
            rows(1), rows(1), rows(4), rows(8),
            pltpu.VMEM((4, 1, R), jnp.int32), pltpu.VMEM((8, 1, R), jnp.int32), pltpu.VMEM((4 * R, 128), jnp.int32),
            pltpu.VMEM((4 * R, 6 * R), BF16), pltpu.VMEM((6 * R, 4 * R), BF16), rows(4, F32), rows(3, F32),
            rows(4), rows(2), rows(1), rows(1), rows(1), rows(1), rows(1), rows(1), rows(1), rows(1),
            rows(2), rows(2), dma((4,)),
        ] + [dma((2, PIECES))] * 8 + [dma((2, 2))] * 2 + [dma((2, PIECES))] * 6 + [dma((8,))] * 2
        + [dma((2,))] * 2 + [dma((2, PARTS))] * 14,
        compiler_params=pltpu.CompilerParams(
            collective_id=0, has_side_effects=True, vmem_limit_bytes=24 * 1024 * 1024),
        cost_estimate=pl.CostEstimate(
            flops=6 * 4 * R * 6 * R * D, bytes_accessed=12 * R * D, transcendentals=24 * R * R),
    )(*[pltpu.with_memory_space_constraint(x, pltpu.HBM)
        for x in (images, texts, image_ids.reshape(1, R), text_ids.reshape(1, R))], logit_scale, logit_bias)
    return image_rows * logit_scale[0], text_rows * logit_scale[0]


def solution(mesh):
    rows = P(("loop", "group"), None)
    ids = P(("loop", "group"))
    return jax.shard_map(
        functools.partial(shards, mesh.shape["loop"]), mesh=mesh,
        in_specs=(rows, rows, ids, ids, P(), P()), out_specs=(rows, rows), check_vma=False)
```

```python
import functools

import jax
import jax.numpy as jnp
from jax import lax
from jax.experimental import pallas as pl
from jax.experimental.pallas import tpu as pltpu
from jax.sharding import PartitionSpec as P

epsilon = 1e-06
MESH = pl.DeviceIdType.MESH
F32, BF16 = jnp.float32, jnp.bfloat16
ROWS_AT_ONCE = 256
PIECES = 2
PARTS = 2


def kernel(
    n_loop, images, texts, image_ids, text_ids, scale, bias, image_out, text_out,
    raw_i, raw_t, img, txt, idi, idt, keys, w, wt, gt, gi,
    t_s, oc_r, d_s, d_r, c_r, z_r, x_s, x_r, h_s, h_r, y_s, y_r,
    load, gx_s, gx_r, g2_s, g2_r, gf_s, gf_r, gz_s, gz_r, go_s, go_r, gy_s, gy_r, gw_s, gw_r, gh_s, gh_r, id_s, id_r,
    ro_s, ro_r, rd_s, rd_r, rc_s, rc_r, rz_s, rz_r, rx_s, rx_r, rh_s, rh_r, rn_s, rn_r, ra_s, ra_r,
):
    R, D = raw_i.shape
    H = R // 2
    loop, group = lax.axis_index("loop"), lax.axis_index("group")
    core = lax.rem(loop, 2)
    x_lo = lax.rem(loop // 2, 2)
    y, x_hi = group // 2, lax.rem(group, 2)
    flip = loop + 2 - 4 * x_lo
    other = (loop + 1 - 2 * core, group)
    x_near = ((flip, group), (flip, group + 1 - 2 * x_hi))
    y_near = ((loop, lax.rem(y + 1, 4) * 2 + x_hi), (loop, lax.rem(y + 3, 4) * 2 + x_hi))
    z_up = (lax.rem(loop + 4, n_loop), group)
    z_down = (lax.rem(loop + n_loop - 4, n_loop), group)
    low, high = x_lo == 0, x_lo == 1

    loads = [
        pltpu.make_async_copy(src, dst, load.at[i])
        for i, (src, dst) in enumerate(
            [(texts, raw_t), (images, raw_i), (text_ids, idt.at[0]), (image_ids, idi.at[0])])
    ]
    for copy in loads:
        copy.start()
    barrier = pltpu.get_barrier_semaphore()

    def signal(*others):
        for device in others:
            pl.semaphore_signal(barrier, inc=1, device_id=device, device_id_type=MESH)

    signal(*x_near, *y_near, z_down)
    pl.when(core == 1)(lambda: signal(other))

    def normalize(rows, block):
        values = rows[...].astype(F32)
        factor = 1.0 / jnp.sqrt(jnp.sum(values * values, axis=-1, keepdims=True) + epsilon)
        block[0:R, :] = (values * factor).astype(BF16)

    def send(src, dst, s, r, device):
        return pltpu.make_async_remote_copy(
            src_ref=src, dst_ref=dst, send_sem=s, recv_sem=r, device_id=device, device_id_type=MESH)

    def half(ref, slot, h, q, count):
        size = H // count
        at = slot * R + h * H + q * size
        return ref.at[pl.ds(at if isinstance(at, int) else pl.multiple_of(at, size), size)]

    def block(ref, slot):
        at = slot * R
        return ref.at[pl.ds(at if isinstance(at, int) else pl.multiple_of(at, R), R)]

    def gx(i, q):
        return send(half(txt, 0, i, q, PIECES), half(txt, 4 + 2 * x_lo + i, i, q, PIECES), gx_s.at[i, q], gx_r.at[i, q], x_near[i])

    def g2(i, q):
        return send(half(txt, 6 * x_lo, 1 - i, q, PIECES), half(txt, 4 + i, 1 - i, q, PIECES), g2_s.at[i, q], g2_r.at[i, q], x_near[i])

    def gf(i, q):
        return send(half(txt, 6 - 2 * x_lo + i, i, q, PIECES), half(txt, 1, i, q, PIECES), gf_s.at[i, q], gf_r.at[i, q], x_near[1 - i])

    def gz(i, q):
        return send(half(txt, (6 + i) * (1 - x_lo), i, q, PIECES), half(txt, 4 + i + x_lo * (2 - i), i, q, PIECES),
                    gz_s.at[i, q], gz_r.at[i, q], z_up)

    def go(i, h):
        return send(half(txt, 4 * core + i, h, 0, 1), half(txt, 2 + i, h, 0, 1), go_s.at[i, h], go_r.at[i, h], other)

    def gy(i, q):
        return send(half(img, 0, i, q, PIECES), half(img, 1 + i, i, q, PIECES), gy_s.at[i, q], gy_r.at[i, q], y_near[i])

    def gw(i, q):
        return send(half(img, 0, 1 - i, q, PIECES), half(img, 1 + i, 1 - i, q, PIECES), gw_s.at[i, q], gw_r.at[i, q], y_near[i])

    def gh(i, q):
        return send(half(img, 1 + i, i, q, PIECES), half(img, 3, i, q, PIECES), gh_s.at[i, q], gh_r.at[i, q], y_near[i])

    def ids(k, src, dst, device):
        return send(src, dst, id_s.at[k], id_r.at[k], device)

    id_x = [ids(i, idt.at[0], idt.at[4 + 2 * x_lo + i], x_near[i]) for i in range(2)]
    id_f = ids(2, idt.at[6 - 2 * x_lo], idt.at[1], x_near[1])
    id_z = ids(3, idt.at[6:8], idt.at[4:6], z_up)
    id_o = ids(4, idt.at[pl.ds(4 * core, 2)], idt.at[2:4], other)
    id_y = [ids(5 + i, idi.at[0], idi.at[1 + i], y_near[i]) for i in range(2)]
    id_h = ids(7, idi.at[1], idi.at[3], y_near[0])

    def pieces(count):
        return [(i, q) for q in range(count) for i in range(2)]

    loads[0].wait()
    normalize(raw_t, txt)
    loads[2].wait()
    loads[3].wait()
    pl.semaphore_wait(barrier, 6 - core)
    for copy in id_x + id_y:
        copy.start()
    for i, q in pieces(PIECES):
        gx(i, q).start()

    @pl.when(low)
    def _():
        for i, q in pieces(PIECES):
            g2(i, q).start()

    @pl.when(high)
    def _():
        for i, q in pieces(PIECES):
            gz(i, q).start()

    loads[1].wait()
    normalize(raw_i, img)
    for i, q in pieces(PIECES):
        gy(i, q).start()
    for i, q in pieces(PIECES):
        gw(i, q).start()

    @pl.when(core == 0)
    def _():
        for h in range(2):
            go(0, h).start()

    def x_step(i, q):
        gx(i, q).wait_recv()
        gf(i, q).start()

        @pl.when(low)
        def _():
            gz(i, q).start()

    def y_step(i, q):
        gy(i, q).wait_recv()
        gh(i, q).start()

    def pass_on(q):
        @pl.when(x_hi == 0)
        def _():
            x_step(1, q)
            x_step(0, q)

        @pl.when(x_hi == 1)
        def _():
            x_step(0, q)
            x_step(1, q)

        @pl.when(y < 2)
        def _():
            y_step(1, q)
            y_step(0, q)

        @pl.when(y >= 2)
        def _():
            y_step(0, q)
            y_step(1, q)

    pass_on(0)
    for copy in id_x + id_y:
        copy.wait_recv()
    id_f.start()
    id_h.start()

    @pl.when(low)
    def _():
        id_z.start()

    for q in range(1, PIECES):
        pass_on(q)

    def pass_sideways(q):
        for i in range(2):
            gz(i, q).wait_recv()
            g2(1 - i, q).start()

    pl.when(high)(lambda: pass_sideways(0))
    pl.when(high & (loop >= 4))(lambda: pass_sideways(1))
    id_f.wait_recv()

    @pl.when(high & (core == 1))
    def _():
        go(0, 0).wait_recv()

    @pl.when(high | (core == 0))
    def _():
        id_o.start()

    @pl.when(high)
    def _():
        for i in range(2):
            for q in range(PIECES):
                g2(i, q).wait_recv()

            @pl.when(core == 1)
            def _():
                for h in range(2):
                    go(i, h).start()

    for i, q in pieces(PIECES):
        gw(i, q).wait_recv()
    for i in range(2):
        for q in range(PIECES):
            gf(i, q).wait_recv()

        @pl.when(core == 0)
        def _():
            go(1, i).start()

    id_h.wait_recv()
    for s in range(4):
        keys[s * R:(s + 1) * R, :] = jnp.transpose(jnp.broadcast_to(idi[s], (128, R)))
    for i, q in pieces(PIECES):
        gh(i, q).wait_recv()

    scale_value, bias_value = scale[0], bias[0]

    def pair(b):
        return pl.ds(b * 2 * R if isinstance(b, int) else pl.multiple_of(b * 2 * R, 2 * R), 2 * R)

    def weigh(b):
        for a in range(4 * R // ROWS_AT_ONCE):
            rows = slice(a * ROWS_AT_ONCE, (a + 1) * ROWS_AT_ONCE)
            dots = lax.dot_general(
                img[rows, :], txt[pair(b), :], (((1,), (1,)), ((), ())), preferred_element_type=F32)
            logits = scale_value * dots + bias_value
            mine = keys[rows, :]
            same = jnp.concatenate([mine == idt[2 * b], mine == idt[2 * b + 1]], axis=1)
            share = jax.nn.sigmoid(jnp.where(same, -logits, logits))
            weights = jnp.where(same, -share, share)
            w[rows, pair(b)] = weights.astype(BF16)
            wt[pair(b), rows] = jnp.transpose(weights).astype(BF16)

    def ro(i):
        return send(block(t_s, i), block(oc_r, i), ro_s.at[i], ro_r.at[i], other)

    def rd(i, q):
        return send(half(d_s, 0, i, q, PARTS), half(d_r, 0, i, q, PARTS), rd_s.at[i, q], rd_r.at[i, q], x_near[1 - i])

    def rc(i, q):
        return send(half(t_s, 2 + i, 1 - i, q, PARTS), half(c_r, 0, 1 - i, q, PARTS), rc_s.at[i, q], rc_r.at[i, q], x_near[i])

    def rz(i, q):
        return send(half(t_s, 2 + i, i, q, PARTS), half(z_r, 0, i, q, PARTS), rz_s.at[i, q], rz_r.at[i, q], z_down)

    def rz_on(i, q):
        return send(half(c_r, 0, i, q, PARTS), half(z_r, 0, i, q, PARTS), rz_s.at[i, q], rz_r.at[i, q], z_down)

    def rx(i, q):
        return send(half(x_s, 0, i, q, PARTS), half(x_r, 0, i, q, PARTS), rx_s.at[i, q], rx_r.at[i, q], x_near[i])

    def rh(i, q):
        return send(half(h_s, 0, i, q, PARTS), half(h_r, 0, i, q, PARTS), rh_s.at[i, q], rh_r.at[i, q], y_near[i])

    def rn(i, q):
        return send(half(y_s, i, 1 - i, q, PARTS), half(y_r, i, 1 - i, q, PARTS), rn_s.at[i, q], rn_r.at[i, q], y_near[i])

    def ra(i, q):
        return send(half(y_s, i, i, q, PARTS), half(y_r, i, i, q, PARTS), ra_s.at[i, q], ra_r.at[i, q], y_near[i])

    def text_part(b):
        return jnp.dot(wt[pair(b), :], img[...], preferred_element_type=F32)

    def image_part(a):
        return jnp.dot(w[a * 2 * R:(a + 1) * 2 * R, :], txt[0:6 * R, :], preferred_element_type=F32)

    def send_far(more=0.0):
        d_s[...] = (gt[R:2 * R, :] + more).astype(BF16)
        for i, q in pieces(PARTS):
            rd(i, q).start()

    def send_cross(i):
        for q in range(PARTS):
            rc(i, q).start()

        @pl.when(low)
        def _():
            for q in range(PARTS):
                rz(i, q).start()

    def from_below():
        id_z.wait_recv()

        @pl.when(core == 1)
        def _():
            go(0, 0).wait_recv()
            id_o.start()

        for i in range(2):
            for q in range(PIECES):
                gz(i, q).wait_recv()

            @pl.when(core == 1)
            def _():
                go(i, i).start()

        for i in range(2):
            for q in range(PIECES):
                g2(i, q).wait_recv()

            @pl.when(core == 1)
            def _():
                go(i, 1 - i).start()

    def from_other():
        id_o.wait_recv()
        pl.when(core == 0)(go(0, 0).wait_recv)
        for i, h in ((0, 1), (1, 0), (1, 1)):
            go(i, h).wait_recv()

    def image_far():
        part = image_part(1)
        h_s[...] = part[R:2 * R].astype(BF16)
        gi[2 * R:3 * R, :] = part[0:R]
        y_s[H:R, :] = part[H:R].astype(BF16)
        for i, q in pieces(PARTS):
            rh(i, q).start()
        for q in range(PARTS):
            rn(0, q).start()

    def image_near():
        part = image_part(0)
        gi[0:2 * R, :] = part
        y_s[R:R + H, :] = part[R:R + H].astype(BF16)
        for q in range(PARTS):
            rn(1, q).start()

    weigh(0)
    gt[0:2 * R, :] = text_part(0)
    pl.when(core == 1)(send_far)
    pl.when(high & (loop < 4))(lambda: pass_sideways(1))
    pl.when(low)(from_below)
    pl.when(core == 1)(from_other)
    weigh(2 - core)
    t_s[pair(1 - core), :] = text_part(2 - core).astype(BF16)

    @pl.when(core == 1)
    def _():
        for i in (1, 0):
            ro(i).start()

    @pl.when(core == 0)
    def _():
        for i in range(2):
            send_cross(i)

    pl.when(core == 0)(from_other)
    weigh(1 + core)
    image_far()

    @pl.when(core == 0)
    def _():
        ro(1).wait_recv()
        send_far(oc_r[R:2 * R, :].astype(F32))

    gt[2 * R:4 * R, :] = text_part(1 + core)

    @pl.when(core == 0)
    def _():
        t_s[0:2 * R, :] = gt[2 * R:4 * R, :].astype(BF16)
        for i in range(2):
            ro(i).start()


    @pl.when(core == 1)
    def _():
        for i in range(2):
            ro(i).wait_recv()
            at = slice((2 + i) * R, (3 + i) * R)
            t_s[at, :] = (gt[at, :] + oc_r[i * R:(i + 1) * R, :].astype(F32)).astype(BF16)
            send_cross(i)

    image_near()

    def piece(h, q):
        return slice(h * H + q * (H // PARTS), h * H + (q + 1) * (H // PARTS))

    def shifted(at, slot):
        return slice(slot * R + at.start, slot * R + at.stop)

    @pl.when(high)
    def _():
        for i, q in pieces(PARTS):
            rc(i, q).wait_recv()
            rz_on(1 - i, q).start()

    for i, q in pieces(PARTS):
        rh(i, q).wait_recv()
        at = piece(i, q)
        y_s[shifted(at, i), :] = (gi[shifted(at, 2 - i), :] + h_r[at, :].astype(F32)).astype(BF16)
        ra(i, q).start()

    def send_near(i, q, first):
        at = piece(i, q)
        x_s[at, :] = (first.astype(F32) + d_r[at, :].astype(F32)).astype(BF16)
        rx(i, q).start()

    for i, q in pieces(PARTS):
        rd(i, q).wait_recv()

        @pl.when(low)
        def _():
            rz(i, q).wait_recv()
            send_near(i, q, z_r[piece(i, q), :])

        @pl.when(high)
        def _():
            send_near(i, q, t_s[shifted(piece(i, q), 2 + i), :])

    def backward(rows, total, out):
        values = rows[...].astype(F32)
        factor = 1.0 / jnp.sqrt(jnp.sum(values * values, axis=-1, keepdims=True) + epsilon)
        unit = values * factor
        grad = total
        along = jnp.sum(unit * grad, axis=-1, keepdims=True)
        out[...] = factor * (grad - unit * along)

    for i, q in pieces(PARTS):
        rn(i, q).wait_recv()
        ra(i, q).wait_recv()
    backward(raw_i, gi[0:R, :] + (y_r[0:R, :].astype(F32) + y_r[R:2 * R, :].astype(F32)), image_out)

    @pl.when(core == 0)
    def _():
        ro(0).wait_recv()
        gt[0:R, :] = gt[0:R, :] + oc_r[0:R, :].astype(F32)

    @pl.when(high)
    def _():
        for i, q in pieces(PARTS):
            rz(i, q).wait_recv()
        gt[R:2 * R, :] = gt[0:R, :] + z_r[...].astype(F32)

    @pl.when(low)
    def _():
        for i, q in pieces(PARTS):
            rc(i, q).wait_recv()
        gt[R:2 * R, :] = gt[0:R, :] + c_r[...].astype(F32)

    for i, q in pieces(PARTS):
        rx(i, q).wait_recv()
    backward(raw_t, gt[R:2 * R, :] + x_r[...].astype(F32), text_out)

    for copy in (gx, g2, gf, gz, gy, gw, gh):
        for i, q in pieces(PIECES):
            copy(i, q).wait_send()
    for copy in (rd, rc, rz, rx, rh, rn, ra):
        for i, q in pieces(PARTS):
            copy(i, q).wait_send()
    for i in range(2):
        for h in range(2):
            go(i, h).wait_send()
        ro(i).wait_send()
    for copy in id_x + id_y + [id_f, id_o, id_h]:
        copy.wait_send()

    @pl.when(low)
    def _():
        id_z.wait_send()


def shards(n_loop, images, texts, image_ids, text_ids, logit_scale, logit_bias):
    R, D = images.shape
    dma = pltpu.SemaphoreType.DMA
    vmem = pl.BlockSpec(memory_space=pltpu.VMEM)
    smem = pl.BlockSpec(memory_space=pltpu.SMEM)
    anywhere = pl.BlockSpec(memory_space=pltpu.HBM)

    def rows(count, dtype=BF16):
        return pltpu.VMEM((count * R, D), dtype)

    image_rows, text_rows = pl.pallas_call(
        functools.partial(kernel, n_loop),
        out_shape=(pltpu.VMEM((R, D), F32), pltpu.VMEM((R, D), F32)),
        in_specs=[anywhere, anywhere, anywhere, anywhere, smem, smem],
        out_specs=(vmem, vmem),
        scratch_shapes=[
            rows(1), rows(1), rows(4), rows(8),
            pltpu.VMEM((4, 1, R), jnp.int32), pltpu.VMEM((8, 1, R), jnp.int32), pltpu.VMEM((4 * R, 128), jnp.int32),
            pltpu.VMEM((4 * R, 6 * R), BF16), pltpu.VMEM((6 * R, 4 * R), BF16), rows(4, F32), rows(3, F32),
            rows(4), rows(2), rows(1), rows(1), rows(1), rows(1), rows(1), rows(1), rows(1), rows(1),
            rows(2), rows(2), dma((4,)),
        ] + [dma((2, PIECES))] * 8 + [dma((2, 2))] * 2 + [dma((2, PIECES))] * 6 + [dma((8,))] * 2
        + [dma((2,))] * 2 + [dma((2, PARTS))] * 14,
        compiler_params=pltpu.CompilerParams(
            collective_id=0, has_side_effects=True, vmem_limit_bytes=24 * 1024 * 1024),
        cost_estimate=pl.CostEstimate(
            flops=6 * 4 * R * 6 * R * D, bytes_accessed=12 * R * D, transcendentals=24 * R * R),
    )(*[pltpu.with_memory_space_constraint(x, pltpu.HBM)
        for x in (images, texts, image_ids.reshape(1, R), text_ids.reshape(1, R))], logit_scale, logit_bias)
    return image_rows * logit_scale[0], text_rows * logit_scale[0]


def solution(mesh):
    rows = P(("loop", "group"), None)
    ids = P(("loop", "group"))
    return jax.shard_map(
        functools.partial(shards, mesh.shape["loop"]), mesh=mesh,
        in_specs=(rows, rows, ids, ids, P(), P()), out_specs=(rows, rows), check_vma=False)
```
